128 devices in a mesh: dp: 16 (over z_hi, x, core), vocab: 8 (over z_lo, y).
Axes of the slice: x: 4, y: 4, z: 4 (z_hi: 2, z_lo: 2; z = z_hi * 2 + z_lo), core: 2. Of those that a mesh axis runs over, the one named last changes fastest.
Arguments:
- hidden: bfloat16 [512, 4608], P('dp'), may hold values from -6 to 6
- head: bfloat16 [4608, 131072], P(None, ('dp', 'vocab')), may hold values from -0.1875 to 0.1875
- verdict_ids: int32 [512], replicated, may hold values from 0 to 131071
- row_weight: float32 [512], replicated, may hold values from 0.5 to 2
Outputs:
- logprob: float32 [512], P('dp')
- head_grad: bfloat16 [4608, 131072], P(None, ('dp', 'vocab'))
- hidden_grad: bfloat16 [512, 4608], P('dp', 'vocab')
The draws below stay inside these ranges and needn't reach their ends.
Inputs may be any that keep to these rules, and one draw needn't show every extreme that they name: `verdict_ids`: each row's verdict token is a column of the whole vocabulary of 131072.
All inputs are finite; a program needn't handle non-finite values.
Results may differ from the reference program's by a relative error of at most 0.02.
Values may be sent and summed in bfloat16 or wider, within the bound.
No kernel may reach another device: no remote copies, remote signals or barrier semaphores. Data moves between devices by JAX's collectives and lax.ppermute only.
A program may use at most 128 MiB of HBM per device.

```python
import jax
import jax.numpy as jnp
from jax import lax

D = 4608
ROWS = 512
VOCAB = 131072


def touch_ends(array, own_key, least, largest):
    extent = array.shape
    spot = [jax.random.randint(jax.random.fold_in(own_key, axis), (), 0, extent[axis]) for axis in range(len(extent))]
    array = array.at[tuple(spot)].set(least)
    longest = extent.index(max(extent))
    spot[longest] = (spot[longest] + 1) % extent[longest]
    return array.at[tuple(spot)].set(largest)


def steps_of(own_key, dims, split, least, top_value):
    def one(position, parts):
        draws = jax.random.uniform(jax.random.fold_in(jax.random.fold_in(own_key, 6), position), (parts,), jnp.float32, least / len(split), top_value / len(split))
        return jnp.repeat(jnp.exp(draws), dims[position] // parts).reshape((-1,) + (1,) * (len(dims) - position - 1))

    level = one(*split[0])
    for cut in split[1:]:
        level = level * one(*cut)
    return level


def centred(rng, shape, spread, most, pieces=(), held_as=jnp.bfloat16):
    factor_of = steps_of(rng, shape, pieces, -0.22, 0.18) if pieces else 1.0
    drawn = jax.random.normal(rng, shape, jnp.float32) * spread * factor_of
    return jnp.minimum(jnp.maximum(drawn, -most), most).astype(held_as)


def setup_inputs(seed: int = 0) -> dict:
    keys = jax.random.split(jax.random.key(seed), 5)
    return {
        "hidden": centred(keys[0], (ROWS, D), 1.0, 6.0, ((0, 16),)),
        "head": centred(keys[1], (D, VOCAB), (D // 4) ** -0.5, 0.1875, ((1, 128),)),
        "verdict_ids": touch_ends(jax.random.randint(keys[2], (ROWS,), 0, VOCAB), jax.random.fold_in(keys[2], 1), 0, VOCAB - 1).astype(jnp.int32),
        "row_weight": jnp.clip(jax.random.uniform(keys[3], (ROWS,), jnp.float32, 0.5, 2.0), 0.5, 2.0),
    }


softcap = 30.0


def reference(hidden, head, verdict_ids, row_weight):
    raw = jnp.dot(hidden, head, preferred_element_type=jnp.float32)
    capped = softcap * jnp.tanh(raw / softcap)
    expo = jnp.exp(capped - softcap)
    total = jnp.sum(expo, axis=1)
    column = jnp.arange(capped.shape[1], dtype=jnp.int32)
    onehot = verdict_ids[:, None] == column[None, :]
    target = jnp.sum(jnp.where(onehot, capped, jnp.float32(0.0)), axis=1)
    log_total = jnp.log(total)
    logprob = target - softcap - log_total
    prob = expo * jnp.exp(-log_total)[:, None]
    slope = 1.0 - (capped / softcap) ** 2
    dlog = (row_weight[:, None] * (prob - onehot.astype(jnp.float32)) * slope).astype(jnp.bfloat16)
    head_grad = lax.dot_general(hidden, dlog, (((0,), (0,)), ((), ())), preferred_element_type=jnp.float32).astype(jnp.bfloat16)
    hidden_grad = lax.dot_general(dlog, head, (((1,), (1,)), ((), ())), preferred_element_type=jnp.float32).astype(jnp.bfloat16)
    return logprob, head_grad, hidden_grad
```

```python
import jax
import jax.numpy as jnp
from jax import lax
from jax.sharding import PartitionSpec as P

softcap = 30.0
AXES = ("dp", "vocab")
bf16 = jnp.bfloat16
f32 = jnp.float32


def flips(core0, core1):
    return [(i, i ^ (core1 if i & 8 else core0)) for i in range(128)]


CORE = flips(8, 8)
X1, X2 = flips(16, 48), flips(48, 16)
Y1, Y2 = flips(1, 3), flips(3, 1)
Z1, Z2 = flips(4, 68), flips(68, 4)
ZH = flips(68, 68)


def send(array, partner):
    return lax.ppermute(array, AXES, partner)


def local(hidden, head, verdict_ids, row_weight):
    width = head.shape[1]
    dp = lax.axis_index("dp")
    vocab = lax.axis_index("vocab")
    core, x, zh = dp & 1, (dp >> 1) & 3, dp >> 3
    zl, y = vocab >> 2, vocab & 3
    zero = jnp.zeros_like(core)
    near = 1 + 2 * core
    far = 3 - 2 * core
    mine = jnp.stack([zero, near, far, zero + 2])
    mate = jnp.stack([zero, far, near, zero + 2])

    def ring(own):
        a1, a2 = send(own, X1), send(own, X2)
        return [own, a1, a2, send(a1, X2)]

    own_half = ring(hidden)
    other_half = ring(send(hidden, ZH))
    halves = [
        jnp.concatenate(half + [send(piece, CORE) for piece in half], axis=0)
        for half in (own_half, other_half)
    ]
    blocks = jnp.concatenate(
        [
            ((zh ^ zr) << 3) | ((x ^ slots) << 1) | c
            for zr in (0, 1)
            for slots, c in ((mine, core), (mate, 1 - core))
        ]
    )
    place = blocks[:, None] == jnp.arange(16, dtype=blocks.dtype)[None, :]

    def to_local(whole):
        return jnp.sum(
            jnp.where(place[:, :, None], whole.reshape(1, 16, 32), jnp.zeros((), whole.dtype)), axis=1
        ).reshape(512)

    def to_whole(part):
        return jnp.sum(jnp.where(place[:, :, None], part.reshape(16, 1, 32), 0.0), axis=0)

    ids = to_local(verdict_ids)
    weight = to_local(row_weight)
    column = (dp * 8 + vocab) * width + jnp.arange(width, dtype=jnp.int32)
    onehot = ids[:, None] == column[None, :]

    capped = []
    for half in halves:
        raw = jnp.dot(half, head, preferred_element_type=f32)
        capped.append(softcap * jnp.tanh(raw / softcap))
    capped = jnp.concatenate(capped, axis=0)
    expo = jnp.exp(capped - softcap)
    partial_total = to_whole(jnp.sum(expo, axis=1))
    partial_target = to_whole(jnp.sum(jnp.where(onehot, capped, 0.0), axis=1))
    parcel = jnp.concatenate(
        [
            jnp.broadcast_to(partial_total.reshape(1, 512), (128, 512)),
            jnp.repeat(partial_target, 8, axis=0),
            jnp.zeros((128, 96), f32),
        ],
        axis=1,
    )
    arrived = lax.all_to_all(parcel.reshape(128, 1, 640), AXES, 0, 0, tiled=True)
    sums = jnp.sum(arrived, axis=(0, 1))
    log_total = jnp.log(sums[:512])
    target = sums[512:544]
    own_log = lax.dynamic_slice_in_dim(log_total, dp * 32, 32, 0)
    logprob = target - softcap - own_log
    log_local = to_local(log_total)
    prob = expo * jnp.exp(-log_local)[:, None]
    slope = 1.0 - (capped / softcap) ** 2
    dlog = (weight[:, None] * (prob - onehot.astype(f32)) * slope).astype(bf16)

    def feature_order(slots):
        return jnp.concatenate([((zl ^ zr) << 2) | (y ^ slots) for zr in (0, 1)])

    head_blocks = head.reshape(8, 576, width)

    def terms(rows, slots):
        ordered = head_blocks[feature_order(slots)].reshape(4608, width)
        return lax.dot_general(rows, ordered, (((1,), (1,)), ((), ())), preferred_element_type=f32)

    by_core = dlog.reshape(2, 2, 128, width)
    for_mate = terms(by_core[:, 1].reshape(256, width), mate).astype(bf16)
    for_me = terms(by_core[:, 0].reshape(256, width), mine).astype(bf16)
    got = send(for_mate, CORE)

    def add(a, b):
        return (a.astype(f32) + b.astype(f32)).astype(bf16)

    summed = add(for_me, got).reshape(2, 4, 32, 2, 2304)
    even = core == 0
    z_slots = jnp.stack(
        [
            summed[0, :, :, 0],
            jnp.where(even, summed[0, :, :, 1], summed[1, :, :, 1]),
            jnp.where(even, summed[1, :, :, 1], summed[0, :, :, 1]),
            summed[1, :, :, 0],
        ]
    )
    p = z_slots[:, :, :16]
    q = z_slots[:, :, 16:]
    p = add(p[:, :2], send(p[:, 2:], X2))
    q = add(q[:2], send(q[2:], Z2))
    p = add(p[:, 0], send(p[:, 1], X1))
    q = add(q[0], send(q[1], Z1))
    p = add(p[:2], send(p[2:], Z2))
    q = add(q[:2], send(q[2:], X2))
    p = add(p[0], send(p[1], Z1))
    q = add(q[0], send(q[1], X1))
    pq = jnp.concatenate([p, q], axis=0)
    pq = add(pq[:, :1152], send(pq[:, 1152:], Y2))
    hidden_grad = add(pq[:, :576], send(pq[:, 576:], Y1))

    gathered = jnp.concatenate(halves, axis=0)
    head_grad = lax.dot_general(
        gathered, dlog, (((0,), (0,)), ((), ())), preferred_element_type=f32
    ).astype(bf16)
    return (logprob, head_grad, hidden_grad)


def solution(mesh):
    in_specs = (P("dp", None), P(None, ("dp", "vocab")), P(), P())
    out_specs = (P("dp"), P(None, ("dp", "vocab")), P("dp", "vocab"))
    return jax.shard_map(local, mesh=mesh, in_specs=in_specs, out_specs=out_specs, check_vma=False)
```

```python
import functools

import jax
import jax.numpy as jnp
from jax import lax
from jax.experimental import pallas as pl
from jax.experimental.pallas import tpu as pltpu
from jax.sharding import PartitionSpec as P

softcap = 30.0
AXES = ("dp", "vocab")
bf16 = jnp.bfloat16
f32 = jnp.float32
D = 4608
WIDTH = 1024
FEATURES = 576


def flips(core0, core1):
    return [(i, i ^ (core1 if i & 8 else core0)) for i in range(128)]


CORE = flips(8, 8)
X1, X2 = flips(16, 48), flips(48, 16)
Y1, Y2 = flips(1, 3), flips(3, 1)
Z1, Z2 = flips(4, 68), flips(68, 4)
ZH = flips(68, 68)


def send(array, partner):
    return lax.ppermute(array, AXES, partner)


def params(mib):
    return pltpu.CompilerParams(vmem_limit_bytes=mib << 20)


def cost(flops, moved):
    return pl.CostEstimate(flops=flops, bytes_accessed=moved, transcendentals=0)


def forward_kernel(base_ref, *refs):
    pieces, (ids_ref, head_ref, capped_ref, total_ref, target_ref, rows, sums, hits) = refs[:8], refs[8:]
    step = pl.program_id(0)

    @pl.when(step == 0)
    def _():
        for i in range(8):
            rows[32 * i : 32 * i + 32, :] = pieces[i][...]
        sums[...] = jnp.zeros_like(sums)
        hits[...] = jnp.zeros_like(hits)

    raw = jnp.dot(rows[...], head_ref[...], preferred_element_type=f32)
    capped = softcap * jnp.tanh(raw / softcap)
    capped_ref[...] = capped
    ids = ids_ref[...]
    lane = lax.broadcasted_iota(jnp.int32, (256, 128), 1)
    total = sums[...]
    hit = hits[...]
    for j in range(2):
        part = capped[:, 128 * j : 128 * j + 128]
        total = total + jnp.exp(part - softcap)
        hit = hit + jnp.where(ids == lane + (base_ref[0] + step * 256 + 128 * j), part, 0.0)
    sums[...] = total
    hits[...] = hit

    @pl.when(step == 3)
    def _():
        total_ref[...] = jnp.sum(total.T, axis=0, keepdims=True)
        target_ref[...] = jnp.sum(hit.T, axis=0, keepdims=True)


def forward(base, pieces, ids, head):
    whole = pl.BlockSpec((32, D), lambda n, *_: (0, 0))
    row = pl.BlockSpec((1, 256), lambda n, *_: (0, 0))
    return pl.pallas_call(
        forward_kernel,
        grid_spec=pltpu.PrefetchScalarGridSpec(
            num_scalar_prefetch=1,
            grid=(4,),
            in_specs=[whole] * 8
            + [
                pl.BlockSpec((256, 128), lambda n, *_: (0, 0)),
                pl.BlockSpec((D, 256), lambda n, *_: (0, n)),
            ],
            out_specs=[pl.BlockSpec((256, 256), lambda n, *_: (0, n)), row, row],
            scratch_shapes=[
                pltpu.VMEM((256, D), bf16),
                pltpu.VMEM((256, 128), f32),
                pltpu.VMEM((256, 128), f32),
            ],
        ),
        out_shape=[
            jax.ShapeDtypeStruct((256, WIDTH), f32),
            jax.ShapeDtypeStruct((1, 256), f32),
            jax.ShapeDtypeStruct((1, 256), f32),
        ],
        compiler_params=params(32),
        cost_estimate=cost(2 * 256 * D * WIDTH, 2 * D * WIDTH),
        name="forward",
    )(base, *pieces, ids, head)


def dlog_kernel(base_ref, low_ref, high_ref, log_ref, weight_ref, ids_ref, out_ref):
    step = pl.program_id(0)
    log_total = jnp.broadcast_to(log_ref[...], (128, 128)).T
    weight = weight_ref[...]
    ids = ids_ref[...]
    lane = lax.broadcasted_iota(jnp.int32, (128, 128), 1)

    def fill(capped_ref):
        for j in range(WIDTH // 128):
            spot = slice(128 * j, 128 * j + 128)
            capped = capped_ref[:, spot]
            prob = jnp.exp(capped - softcap - log_total)
            onehot = jnp.where(ids == lane + (base_ref[0] + 128 * j), 1.0, 0.0)
            ratio = capped / softcap
            out_ref[:, spot] = (weight * (prob - onehot) * (1.0 - ratio * ratio)).astype(bf16)

    @pl.when(step < 2)
    def _():
        fill(low_ref)

    @pl.when(step >= 2)
    def _():
        fill(high_ref)


def dlogits(base, low, high, log_total, weight, ids):
    column = pl.BlockSpec((128, 128), lambda n, *_: (n, 0))
    return pl.pallas_call(
        dlog_kernel,
        grid_spec=pltpu.PrefetchScalarGridSpec(
            num_scalar_prefetch=1,
            grid=(4,),
            in_specs=[
                pl.BlockSpec((128, WIDTH), lambda n, *_: (jnp.minimum(n, 1), 0)),
                pl.BlockSpec((128, WIDTH), lambda n, *_: (jnp.maximum(n - 2, 0), 0)),
                pl.BlockSpec((1, 128), lambda n, *_: (0, n)),
                column,
                column,
            ],
            out_specs=pl.BlockSpec((128, WIDTH), lambda n, *_: (n, 0)),
        ),
        out_shape=jax.ShapeDtypeStruct((512, WIDTH), bf16),
        compiler_params=params(24),
        cost_estimate=cost(512 * WIDTH * 16, 6 * 512 * WIDTH),
        name="dlog",
    )(base, low, high, log_total, weight, ids)


def product(dlog0, dlog1, head0, head1):
    rows = jnp.concatenate([dlog0[...], dlog1[...]], axis=0)
    features = jnp.concatenate([head0[...], head1[...]], axis=0)
    return lax.dot_general(rows, features, (((1,), (1,)), ((), ())), preferred_element_type=f32)


def mate_kernel(order_ref, dlog0, dlog1, head0, head1, out_ref):
    out_ref[...] = product(dlog0, dlog1, head0, head1).astype(bf16)


def mine_kernel(order_ref, dlog0, dlog1, head0, head1, got_ref, p_keep, p_send, q_keep, q_send, total):
    total[...] = product(dlog0, dlog1, head0, head1) + got_ref[...].astype(f32)
    for z in range(2):
        half = order_ref[8] if z == 0 else 1 - order_ref[8]
        for x in range(4):
            start = pl.multiple_of(half * 128, 128) + 32 * x
            (p_keep if x < 2 else p_send)[z, x % 2] = total[pl.ds(start, 16), :].astype(bf16)
            (q_keep if z == 0 else q_send)[x] = total[pl.ds(start + 16, 16), :].astype(bf16)


def hidden_specs(half, own):
    def rows(zr):
        return pl.BlockSpec((128, WIDTH), lambda n, *_: (2 * zr + 1 - own, 0))

    def block(i):
        return pl.BlockSpec((FEATURES, WIDTH), lambda n, order: (order[4 * half + 2 * n + i], 0))

    return [rows(0), rows(1), block(0), block(1)]


HALF_COST = 2 * 256 * WIDTH * D // 2


def mate_terms(half, order, dlog, head):
    return pl.pallas_call(
        mate_kernel,
        grid_spec=pltpu.PrefetchScalarGridSpec(
            num_scalar_prefetch=1,
            grid=(2,),
            in_specs=hidden_specs(half, 0),
            out_specs=pl.BlockSpec((256, 1152), lambda n, *_: (0, n)),
        ),
        out_shape=jax.ShapeDtypeStruct((256, 2304), bf16),
        compiler_params=params(32),
        cost_estimate=cost(HALF_COST, D * WIDTH),
        name="mate_terms",
    )(order, dlog, dlog, head, head)


def mine_terms(half, order, dlog, head, got):
    p_spec = pl.BlockSpec((2, 2, 16, 1152), lambda n, *_: (0, 0, 0, n))
    q_spec = pl.BlockSpec((4, 16, 1152), lambda n, *_: (0, 0, n))
    p_shape = jax.ShapeDtypeStruct((2, 2, 16, 2304), bf16)
    q_shape = jax.ShapeDtypeStruct((4, 16, 2304), bf16)
    return pl.pallas_call(
        mine_kernel,
        grid_spec=pltpu.PrefetchScalarGridSpec(
            num_scalar_prefetch=1,
            grid=(2,),
            in_specs=hidden_specs(half, 1) + [pl.BlockSpec((256, 1152), lambda n, *_: (0, n))],
            out_specs=[p_spec, p_spec, q_spec, q_spec],
            scratch_shapes=[pltpu.VMEM((256, 1152), f32)],
        ),
        out_shape=[p_shape, p_shape, q_shape, q_shape],
        compiler_params=params(32),
        cost_estimate=cost(HALF_COST, D * WIDTH),
        name="mine_terms",
    )(order, dlog, dlog, head, head, got)


def head_grad_kernel(*refs):
    pieces, (dlog_ref, out_ref) = refs[:16], refs[16:]
    rows = jnp.concatenate([piece[...] for piece in pieces], axis=0)
    out_ref[...] = lax.dot_general(
        rows, dlog_ref[...], (((0,), (0,)), ((), ())), preferred_element_type=f32
    ).astype(bf16)


def head_gradient(pieces, dlog):
    return pl.pallas_call(
        head_grad_kernel,
        grid=(9,),
        in_specs=[pl.BlockSpec((32, 512), lambda n: (0, n))] * 16
        + [pl.BlockSpec((512, WIDTH), lambda n: (0, 0))],
        out_specs=pl.BlockSpec((512, WIDTH), lambda n: (n, 0)),
        out_shape=jax.ShapeDtypeStruct((D, WIDTH), bf16),
        compiler_params=params(32),
        cost_estimate=cost(2 * 512 * WIDTH * D, 2 * D * WIDTH),
        name="head_gradient",
    )(*pieces, dlog)


def local(hidden, head, verdict_ids, row_weight):
    width = head.shape[1]
    dp = lax.axis_index("dp")
    vocab = lax.axis_index("vocab")
    core, x, zh = dp & 1, (dp >> 1) & 3, dp >> 3
    zl, y = vocab >> 2, vocab & 3
    zero = jnp.zeros_like(core)
    near = 1 + 2 * core
    far = 3 - 2 * core
    mine = jnp.stack([zero, near, far, zero + 2])
    mate = jnp.stack([zero, far, near, zero + 2])

    def ring(own):
        a1, a2 = send(own, X1), send(own, X2)
        return [own, a1, a2, send(a1, X2)]

    own_half = ring(hidden)
    other_half = ring(send(hidden, ZH))
    halves = [half + [send(piece, CORE) for piece in half] for half in (own_half, other_half)]
    blocks = jnp.concatenate(
        [
            ((zh ^ zr) << 3) | ((x ^ slots) << 1) | c
            for zr in (0, 1)
            for slots, c in ((mine, core), (mate, 1 - core))
        ]
    )
    place = blocks[:, None] == jnp.arange(16, dtype=blocks.dtype)[None, :]

    def to_local(whole):
        return jnp.sum(
            jnp.where(place[:, :, None], whole.reshape(1, 16, 32), jnp.zeros((), whole.dtype)), axis=1
        ).reshape(512)

    def to_whole(part):
        return jnp.sum(jnp.where(place[:, :, None], part.reshape(16, 1, 32), 0.0), axis=0)

    def order_of(slots, second):
        blocks_of = [((zl ^ zr) << 2) | (y ^ slots) for zr in (0, 1)]
        return jnp.concatenate(blocks_of + [jnp.stack([second])]).astype(jnp.int32)

    ids = jnp.broadcast_to(to_local(verdict_ids)[:, None], (512, 128))
    weight = jnp.broadcast_to(to_local(row_weight)[:, None], (512, 128))
    base = ((dp * 8 + vocab) * width).astype(jnp.int32).reshape(1)

    capped0, total0, target0 = forward(base, halves[0], ids[:256], head)
    capped1, total1, target1 = forward(base, halves[1], ids[256:], head)
    partial_total = to_whole(jnp.concatenate([total0, total1], axis=1))
    partial_target = to_whole(jnp.concatenate([target0, target1], axis=1))
    parcel = jnp.concatenate(
        [
            jnp.broadcast_to(partial_total.reshape(1, 512), (128, 512)),
            jnp.repeat(partial_target, 8, axis=0),
            jnp.zeros((128, 96), f32),
        ],
        axis=1,
    )
    arrived = lax.all_to_all(parcel.reshape(128, 1, 640), AXES, 0, 0, tiled=True)
    sums = jnp.sum(arrived, axis=(0, 1))
    log_total = jnp.log(sums[:512])
    target = sums[512:544]
    own_log = lax.dynamic_slice_in_dim(log_total, dp * 32, 32, 0)
    logprob = target - softcap - own_log
    dlog = dlogits(base, capped0, capped1, to_local(log_total).reshape(1, 512), weight, ids)

    mate_order = order_of(mate, zero)
    mine_order = order_of(mine, zero)
    turned_order = order_of(mine, core)
    got_a = send(mate_terms(0, mate_order, dlog, head), CORE)
    got_b = send(mate_terms(1, mate_order, dlog, head), CORE)
    pa_keep, pa_send, qa_keep, qa_send = mine_terms(0, mine_order, dlog, head, got_a)
    pb_keep, pb_send, qb_keep, qb_send = mine_terms(1, turned_order, dlog, head, got_b)

    def add(a, b):
        return (a.astype(f32) + b.astype(f32)).astype(bf16)

    pa = add(pa_keep, send(pa_send, X2))
    qa_got = send(qa_send, Z2)
    pb = add(pb_keep, send(pb_send, X2))
    qb_got = send(qb_send, Z2)
    q0, q1 = add(qa_keep, qb_got), add(qb_keep, qa_got)
    p_got = send(jnp.concatenate([pa[:, 1], pb[:, 1]], axis=0), X1)
    q = add(q0, send(q1, Z1))
    pa = add(pa[:, 0], p_got[:2])
    pb = add(pb[:, 0], p_got[2:])
    p_got = send(jnp.stack([pb[1], pa[1]]), Z2)
    q = add(q[:2], send(q[2:], X2))
    p0, p1 = add(pa[0], p_got[0]), add(pb[0], p_got[1])
    p = add(p0, send(p1, Z1))
    q = add(q[0], send(q[1], X1))
    pq = jnp.concatenate([p, q], axis=0)
    pq = add(pq[:, :1152], send(pq[:, 1152:], Y2))
    hidden_grad = add(pq[:, :576], send(pq[:, 576:], Y1))

    head_grad = head_gradient(halves[0] + halves[1], dlog)
    return (logprob, head_grad, hidden_grad)


def solution(mesh):
    in_specs = (P("dp", None), P(None, ("dp", "vocab")), P(), P())
    out_specs = (P("dp"), P(None, ("dp", "vocab")), P("dp", "vocab"))
    return jax.shard_map(local, mesh=mesh, in_specs=in_specs, out_specs=out_specs, check_vma=False)
```

```python
import jax
import jax.numpy as jnp
from jax import lax
from jax.experimental import pallas as pl
from jax.experimental.pallas import tpu as pltpu
from jax.sharding import PartitionSpec as P

softcap = 30.0
AXES = ("dp", "vocab")
bf16 = jnp.bfloat16
f32 = jnp.float32
D = 4608
WIDTH = 1024
FEATURES = 576


def flips(core0, core1):
    return [(i, i ^ (core1 if i & 8 else core0)) for i in range(128)]


CORE = flips(8, 8)
X1, X2 = flips(16, 48), flips(48, 16)
Y1, Y2 = flips(1, 3), flips(3, 1)
ZL, ZH = flips(4, 4), flips(68, 68)


def send(array, partner):
    return lax.ppermute(array, AXES, partner)


def call(kernel, ins, outs, scratch=(), flops=0, moved=0, mib=16):
    places = {"v": pltpu.VMEM, "s": pltpu.SMEM, "h": pl.ANY}
    return pl.pallas_call(
        kernel,
        in_specs=[pl.BlockSpec(memory_space=places[i]) for i in ins],
        out_specs=[pl.BlockSpec(memory_space=places[o[0]]) for o in outs],
        out_shape=[jax.ShapeDtypeStruct(o[1], o[2]) for o in outs],
        scratch_shapes=list(scratch),
        compiler_params=pltpu.CompilerParams(vmem_limit_bytes=mib << 20),
        cost_estimate=pl.CostEstimate(flops=flops, bytes_accessed=moved, transcendentals=0),
        name=kernel.__name__,
    )


def forward(base_ref, *refs):
    pieces, (ids_ref, head_ref, rows, capped_ref, term_ref, total_ref, target_ref) = refs[:8], refs[8:]
    for i in range(8):
        rows[32 * i : 32 * i + 32, :] = pieces[i][...]
    ids = ids_ref[...]
    lane = lax.broadcasted_iota(jnp.int32, (256, 128), 1)
    total = jnp.zeros((256, 128), f32)
    hits = jnp.zeros((256, 128), f32)
    for n in range(4):
        raw = jnp.dot(rows[...], head_ref[:, 256 * n : 256 * n + 256], preferred_element_type=f32)
        ratio = jnp.tanh(raw / softcap)
        for j in range(2):
            start = 256 * n + 128 * j
            part = ratio[:, 128 * j : 128 * j + 128]
            capped = softcap * part
            expo = jnp.exp(capped)
            hit = ids == lane + (base_ref[0] + start)
            capped_ref[:, start : start + 128] = capped
            term_ref[:, start : start + 128] = jnp.where(hit, 0.0, expo * (1.0 - part * part)).astype(bf16)
            total = total + expo
            hits = hits + jnp.where(hit, capped, 0.0)
    total_ref[...] = jnp.sum(total.T, axis=0, keepdims=True)
    target_ref[...] = jnp.sum(hits.T, axis=0, keepdims=True)


def run_forward(base, pieces, ids, head):
    return call(
        forward,
        "s" + "v" * 10,
        [
            ("v", (256, D), bf16),
            ("v", (256, WIDTH), f32),
            ("v", (256, WIDTH), bf16),
            ("v", (1, 256), f32),
            ("v", (1, 256), f32),
        ],
        flops=2 * 256 * D * WIDTH,
        moved=2 * D * WIDTH,
    )(base, *pieces, ids, head)


def picks(base_ref, ids_ref, out_ref):
    ids = ids_ref[...]
    lane = lax.broadcasted_iota(jnp.int32, (256, 128), 1)
    for j in range(WIDTH // 128):
        hit = ids == lane + (base_ref[0] + 128 * j)
        out_ref[:, 128 * j : 128 * j + 128] = jnp.where(hit, 1.0, 0.0).astype(bf16)


def run_picks(base, ids):
    return call(picks, "sv", [("v", (256, WIDTH), bf16)], moved=256 * WIDTH * 2)(base, ids)[0]


def back(slot_ref, rows_ref, head_ref, mine_ref, mate_ref):
    for n in range(4):
        out = lax.dot_general(
            rows_ref[...],
            head_ref[1152 * n : 1152 * n + 1152, :],
            (((1,), (1,)), ((), ())),
            preferred_element_type=f32,
        ).astype(bf16)
        for i in range(2):
            part = out[:, FEATURES * i : FEATURES * i + FEATURES]
            mine_ref[slot_ref[2 * n + i]] = part[:128].reshape(4, 32, FEATURES)
            mate_ref[slot_ref[8 + 2 * n + i]] = part[128:].reshape(4, 32, FEATURES)


def run_back(slots, rows, head):
    out = ("v", (8, 4, 32, FEATURES), bf16)
    return call(back, "svv", [out, out], flops=2 * 256 * D * WIDTH, moved=2 * D * WIDTH)(slots, rows, head)


def fold(mine0, got0, mine1, got1, p_keep, p_send, q_keep, q_send):
    for zr, (mine, got) in enumerate(((mine0, got0), (mine1, got1))):
        for zl in range(2):
            for k in range(4):
                total = mine[4 * zl + k].astype(f32) + got[4 * zl + k].astype(f32)
                total = total.astype(bf16)
                (p_keep if k < 2 else p_send)[zr, zl, k % 2] = total[:, :16]
                q_keep[zr, zl, k] = total[:2, 16:]
                q_send[zr, zl, k] = total[2:, 16:]


def run_fold(mine0, got0, mine1, got1):
    p = ("v", (2, 2, 2, 4, 16, FEATURES), bf16)
    q = ("v", (2, 2, 4, 2, 16, FEATURES), bf16)
    return call(fold, "vvvv", [p, p, q, q], moved=512 * D * 4)(mine0, got0, mine1, got1)


def fold_picks(mine0, got0, mine1, got1, keep, out):
    for zr, (mine, got) in enumerate(((mine0, got0), (mine1, got1))):
        for zl in range(2):
            for k in range(4):
                total = mine[4 * zl + k].astype(f32) + got[4 * zl + k].astype(f32)
                (keep if k < 2 else out)[zr, zl, k % 2] = total.astype(bf16)


def run_fold_picks(mine0, got0, mine1, got1):
    p = ("v", (2, 2, 2, 4, 32, FEATURES), bf16)
    return call(fold_picks, "vvvv", [p, p], moved=512 * D * 4)(mine0, got0, mine1, got1)


def dlogits(base_ref, low_ref, high_ref, log_ref, weight_ref, ids_ref, out_ref):
    lane = lax.broadcasted_iota(jnp.int32, (128, 128), 1)
    for n in range(4):
        capped_ref = low_ref if n < 2 else high_ref
        rows = slice(128 * (n % 2), 128 * (n % 2) + 128)
        out_rows = slice(128 * n, 128 * n + 128)
        log_total = jnp.broadcast_to(log_ref[:, out_rows], (128, 128)).T
        weight = weight_ref[out_rows, :]
        ids = ids_ref[out_rows, :]
        for j in range(WIDTH // 128):
            spot = slice(128 * j, 128 * j + 128)
            capped = capped_ref[rows, spot]
            prob = jnp.exp(capped - log_total)
            onehot = jnp.where(ids == lane + (base_ref[0] + 128 * j), 1.0, 0.0)
            ratio = capped / softcap
            out_ref[out_rows, spot] = (weight * (prob - onehot) * (1.0 - ratio * ratio)).astype(bf16)


def run_dlogits(base, low, high, log_total, weight, ids):
    return call(
        dlogits, "svvvvv", [("v", (512, WIDTH), bf16)], flops=512 * WIDTH * 16, moved=6 * 512 * WIDTH
    )(base, low, high, log_total, weight, ids)[0]


def head_gradient(low_ref, high_ref, dlog_ref, out_ref, rows, buffer, sems):
    def copy(i):
        return pltpu.make_async_copy(buffer.at[i % 2], out_ref.at[pl.ds(512 * i, 512)], sems.at[i % 2])

    for i in range(9):
        spot = slice(512 * i, 512 * i + 512)
        rows[:256, :] = low_ref[:, spot]
        rows[256:, :] = high_ref[:, spot]
        if i >= 2:
            copy(i - 2).wait()
        buffer[i % 2] = lax.dot_general(
            rows[...], dlog_ref[...], (((0,), (0,)), ((), ())), preferred_element_type=f32
        ).astype(bf16)
        copy(i).start()
    copy(7).wait()
    copy(8).wait()


def run_head_gradient(low, high, dlog):
    return call(
        head_gradient,
        "vvv",
        [("h", (D, WIDTH), bf16)],
        scratch=[
            pltpu.VMEM((512, 512), bf16),
            pltpu.VMEM((2, 512, WIDTH), bf16),
            pltpu.SemaphoreType.DMA((2,)),
        ],
        flops=2 * 512 * WIDTH * D,
        moved=2 * D * WIDTH,
    )(low, high, dlog)[0]


def add(a, b):
    return (a.astype(f32) + b.astype(f32)).astype(bf16)


def local(hidden, head, verdict_ids, row_weight):
    dp = lax.axis_index("dp")
    vocab = lax.axis_index("vocab")
    core, x, zh = dp & 1, (dp >> 1) & 3, dp >> 3
    zl, y = vocab >> 2, vocab & 3
    zero = jnp.zeros_like(core)
    near = 1 + 2 * core
    far = 3 - 2 * core
    mine = jnp.stack([zero, near, far, zero + 2])
    mate = jnp.stack([zero, far, near, zero + 2])

    def ring(own):
        a1, a2 = send(own, X1), send(own, X2)
        return [own, a1, a2, send(a1, X2)]

    own_half = ring(hidden)
    other_half = ring(send(hidden, ZH))
    halves = [half + [send(piece, CORE) for piece in half] for half in (own_half, other_half)]
    blocks = jnp.concatenate(
        [
            ((zh ^ zr) << 3) | ((x ^ slots) << 1) | c
            for zr in (0, 1)
            for slots, c in ((mine, core), (mate, 1 - core))
        ]
    )
    place = blocks[:, None] == jnp.arange(16, dtype=blocks.dtype)[None, :]

    def to_local(whole):
        return jnp.sum(
            jnp.where(place[:, :, None], whole.reshape(1, 16, 32), jnp.zeros((), whole.dtype)), axis=1
        ).reshape(512)

    def to_whole(part):
        return jnp.sum(jnp.where(place[:, :, None], part.reshape(16, 1, 32), 0.0), axis=0).reshape(512)

    block = jnp.arange(8, dtype=jnp.int32)
    apart = (block & 3) ^ y

    def slots_of(first, second):
        slot = jnp.where(apart == first, 1, jnp.where(apart == second, 2, jnp.where(apart == 2, 3, 0)))
        return ((block >> 2) ^ zl) * 4 + slot

    slots = jnp.concatenate([slots_of(near, far), slots_of(far, near)]).astype(jnp.int32)
    ids = jnp.broadcast_to(to_local(verdict_ids)[:, None], (512, 128))
    weight = jnp.broadcast_to(to_local(row_weight)[:, None], (512, 128))
    base = ((dp * 8 + vocab) * WIDTH).astype(jnp.int32).reshape(1)

    g0_mine, g0_mate = run_back(slots, run_picks(base, ids[:256]), head)
    g0_got = send(g0_mate, CORE)
    g1_mine, g1_mate = run_back(slots, run_picks(base, ids[256:]), head)
    g1_got = send(g1_mate, CORE)
    g_keep, g_send = run_fold_picks(g0_mine, g0_got, g1_mine, g1_got)
    g = add(g_keep, send(g_send, Y2))
    g = add(g[:, :, 0], send(g[:, :, 1], Y1))
    g = add(g[:, :, :2], send(g[:, :, 2:], X2))
    g = add(g[:, :, 0], send(g[:, :, 1], X1))

    rows0, capped0, term0, total0, target0 = run_forward(base, halves[0], ids[:256], head)
    a0_mine, a0_mate = run_back(slots, term0, head)
    a0_got = send(a0_mate, CORE)
    rows1, capped1, term1, total1, target1 = run_forward(base, halves[1], ids[256:], head)
    a1_mine, a1_mate = run_back(slots, term1, head)
    a1_got = send(a1_mate, CORE)
    p_keep, p_send, q_keep, q_send = run_fold(a0_mine, a0_got, a1_mine, a1_got)

    p = add(p_keep, send(p_send, Y2))
    q = add(q_keep, send(q_send, X2))
    p = add(p[:, :, 0], send(p[:, :, 1], Y1))
    q = add(q[:, :, :, 0], send(q[:, :, :, 1], X1))
    p = add(p[:, :, :2], send(p[:, :, 2:], X2))
    q = add(q[:, :, :2], send(q[:, :, 2:], Y2))
    p = add(p[:, :, 0], send(p[:, :, 1], X1))
    q = add(q[:, :, 0], send(q[:, :, 1], Y1))

    pair = jnp.stack(
        [
            to_whole(jnp.concatenate([total0, total1], axis=1)),
            to_whole(jnp.concatenate([target0, target1], axis=1)),
        ]
    ).reshape(8, 128)
    for partner in (CORE, Y1, Y2, X1, X2, ZL, ZH):
        pair = pair + send(pair, partner)
    sums = pair.reshape(2, 512)
    log_total = jnp.log(sums[0])
    own_log = lax.dynamic_slice_in_dim(log_total, dp * 32, 32, 0)
    own_target = lax.dynamic_slice_in_dim(sums[1], dp * 32, 32, 0)
    own_weight = lax.dynamic_slice_in_dim(row_weight, dp * 32, 32, 0)
    logprob = own_target - own_log
    dlog = run_dlogits(base, capped0, capped1, to_local(log_total).reshape(1, 512), weight, ids)
    head_grad = run_head_gradient(rows0, rows1, dlog)

    both = jnp.concatenate([p, q, g], axis=2)
    both = add(both[0], send(both[1], ZH)[::-1])
    both = both[0].astype(f32) + send(both[1], ZL).astype(f32)
    ratio = own_target / softcap
    for_pick = own_weight * (jnp.exp(logprob) - 1.0) * (1.0 - ratio * ratio)
    for_rest = own_weight * jnp.exp(-own_log)
    hidden_grad = (for_rest[:, None] * both[:32] + for_pick[:, None] * both[32:]).astype(bf16)
    return (logprob, head_grad, hidden_grad)


def solution(mesh):
    in_specs = (P("dp", None), P(None, ("dp", "vocab")), P(), P())
    out_specs = (P("dp"), P(None, ("dp", "vocab")), P("dp", "vocab"))
    return jax.shard_map(local, mesh=mesh, in_specs=in_specs, out_specs=out_specs, check_vma=False)
```

```python
import jax
import jax.numpy as jnp
from jax import lax
from jax.experimental import pallas as pl
from jax.experimental.pallas import tpu as pltpu
from jax.sharding import PartitionSpec as P

softcap = 30.0
AXES = ("dp", "vocab")
bf16 = jnp.bfloat16
f32 = jnp.float32
D = 4608
WIDTH = 1024
FEATURES = 576
COLUMN = (512, 128)


def flips(core0, core1):
    return [(i, i ^ (core1 if i & 8 else core0)) for i in range(128)]


CORE = flips(8, 8)
X1, X2 = flips(16, 48), flips(48, 16)
Y1, Y2 = flips(1, 3), flips(3, 1)
ZL, ZH = flips(4, 4), flips(68, 68)


def send(array, partner):
    return lax.ppermute(array, AXES, partner)


def slot_flip(slot, core):
    return (0, 1 + 2 * core, 3 - 2 * core, 2)[slot]


def whole_block(me, i):
    core = ((me >> 3) & 1) ^ ((i >> 2) & 1)
    x = ((me >> 4) & 3) ^ slot_flip(i & 3, core)
    return ((me >> 6) ^ (i >> 3)) * 8 + x * 2 + core


def feature_slot(me, i, other):
    core = ((me >> 3) & 1) ^ other
    apart = (me & 3) ^ (i & 3)
    slot = jnp.where(apart == 1 + 2 * core, 1, jnp.where(apart == 3 - 2 * core, 2, jnp.where(apart == 2, 3, 0)))
    return (((me >> 2) & 1) ^ (i >> 2)) * 4 + slot


def call(kernel, ins, outs, scratch=(), flops=0, moved=0, mib=16):
    places = {"v": pltpu.VMEM, "s": pltpu.SMEM, "h": pl.ANY}
    return pl.pallas_call(
        kernel,
        in_specs=[pl.BlockSpec(memory_space=places[i]) for i in ins],
        out_specs=[pl.BlockSpec(memory_space=places[o[0]]) for o in outs],
        out_shape=[jax.ShapeDtypeStruct(o[1], o[2]) for o in outs],
        scratch_shapes=list(scratch),
        compiler_params=pltpu.CompilerParams(vmem_limit_bytes=mib << 20),
        cost_estimate=pl.CostEstimate(flops=flops, bytes_accessed=moved, transcendentals=0),
        name=kernel.__name__,
    )


def rows_of(i):
    return slice(32 * i, 32 * i + 32)


def from_lanes(row):
    return jnp.broadcast_to(row, (128, 128)).T


def local_block(me, i, whole):
    return whole[pl.ds(pl.multiple_of(whole_block(me, i) * 32, 32), 32), :]


def spread(me_ref, ids_ref, weight_ref, ids_out, weight_out, ids_whole, weight_whole):
    me = me_ref[0]
    for j in range(4):
        ids_whole[128 * j : 128 * j + 128, :] = from_lanes(ids_ref[j : j + 1, :])
        weight_whole[128 * j : 128 * j + 128, :] = from_lanes(weight_ref[j : j + 1, :])
    for i in range(16):
        ids_out[rows_of(i), :] = local_block(me, i, ids_whole)
        weight_out[rows_of(i), :] = local_block(me, i, weight_whole)


def run_spread(me, ids, weight):
    column = ("v", COLUMN, f32)
    return call(spread, "svv", [column, column], scratch=[pltpu.VMEM(COLUMN, f32)] * 2, moved=1 << 20)(me, ids, weight)


def hits_of(me, ids, j):
    lane = lax.broadcasted_iota(jnp.int32, (ids.shape[0], 128), 1)
    return ids == (lane + (me * WIDTH + 128 * j)).astype(f32)


def forward(half, me_ref, *refs):
    pieces, (ids_ref, head_ref, rows, capped_ref, term_ref, total_ref, target_ref) = refs[:8], refs[8:]
    me = me_ref[0]
    for i in range(8):
        rows[rows_of(i), :] = pieces[i][...]
    ids = ids_ref[256 * half : 256 * half + 256, :]
    total = jnp.zeros((256, 128), f32)
    target = jnp.zeros((256, 128), f32)
    for n in range(4):
        raw = jnp.dot(rows[...], head_ref[:, 256 * n : 256 * n + 256], preferred_element_type=f32)
        ratio = jnp.tanh(raw / softcap)
        for j in range(2):
            start = 256 * n + 128 * j
            part = ratio[:, 128 * j : 128 * j + 128]
            capped = softcap * part
            expo = jnp.exp(capped)
            hit = hits_of(me, ids, 2 * n + j)
            capped_ref[:, start : start + 128] = capped
            term_ref[:, start : start + 128] = jnp.where(hit, 0.0, expo * (1.0 - part * part)).astype(bf16)
            total = total + expo
            target = target + jnp.where(hit, capped, 0.0)
    total_ref[...] = total
    target_ref[...] = target


def forward_low(*refs):
    forward(0, *refs)


def forward_high(*refs):
    forward(1, *refs)


def run_forward(kernel, me, pieces, ids, head):
    return call(
        kernel,
        "s" + "v" * 10,
        [
            ("v", (256, D), bf16),
            ("v", (256, WIDTH), f32),
            ("v", (256, WIDTH), bf16),
            ("v", (256, 128), f32),
            ("v", (256, 128), f32),
        ],
        flops=2 * 256 * D * WIDTH,
        moved=2 * D * WIDTH,
    )(me, *pieces, ids, head)


def pack(me_ref, total0, total1, target0, target1, out_ref, whole):
    me = me_ref[0]
    sums = []
    for halves in ((total0, total1), (target0, target1)):
        for i in range(16):
            spot = pl.ds(pl.multiple_of(whole_block(me, i) * 32, 32), 32)
            whole[spot, :] = halves[i // 8][rows_of(i % 8), :]
        for j in range(4):
            sums.append(jnp.sum(whole[128 * j : 128 * j + 128, :].T, axis=0, keepdims=True))
    out_ref[...] = jnp.broadcast_to(jnp.concatenate(sums, axis=0)[None], (128, 8, 128))


def run_pack(me, *columns):
    return call(pack, "svvvv", [("v", (128, 8, 128), f32)], scratch=[pltpu.VMEM(COLUMN, f32)], moved=1 << 20)(
        me, *columns
    )[0]


def unpack(me_ref, arrived_ref, weight_ref, log_ref, own_ref, rest_ref, pick_ref, logs, targets):
    me = me_ref[0]
    sums = jnp.sum(arrived_ref[...], axis=0)
    for j in range(4):
        logs[128 * j : 128 * j + 128, :] = from_lanes(jnp.log(sums[j : j + 1, :]))
        targets[128 * j : 128 * j + 128, :] = from_lanes(sums[4 + j : 5 + j, :])
    for i in range(16):
        log_ref[rows_of(i), :] = local_block(me, i, logs)
    log_total = local_block(me, 0, logs)
    target = local_block(me, 0, targets)
    weight = weight_ref[rows_of(0), :]
    ratio = target / softcap
    own_ref[...] = target - log_total
    rest_ref[...] = weight * jnp.exp(-log_total)
    pick_ref[...] = weight * (jnp.exp(target - log_total) - 1.0) * (1.0 - ratio * ratio)


def run_unpack(me, arrived, weight):
    own = ("v", (32, 128), f32)
    return call(
        unpack, "svv", [("v", COLUMN, f32), own, own, own], scratch=[pltpu.VMEM(COLUMN, f32)] * 2, moved=1 << 20
    )(me, arrived, weight)


def back(me_ref, rows_ref, head_ref, mine_ref, mate_ref):
    me = me_ref[0]
    for n in range(4):
        out = lax.dot_general(
            rows_ref[...],
            head_ref[1152 * n : 1152 * n + 1152, :],
            (((1,), (1,)), ((), ())),
            preferred_element_type=f32,
        ).astype(bf16)
        for i in range(2):
            part = out[:, FEATURES * i : FEATURES * i + FEATURES]
            mine_ref[feature_slot(me, 2 * n + i, 0)] = part[:128].reshape(4, 32, FEATURES)
            mate_ref[feature_slot(me, 2 * n + i, 1)] = part[128:].reshape(4, 32, FEATURES)


BLOCKS = ("v", (8, 4, 32, FEATURES), bf16)
BACK_COST = dict(flops=2 * 256 * D * WIDTH, moved=2 * D * WIDTH)


def run_back(me, rows, head):
    return call(back, "svv", [BLOCKS, BLOCKS], **BACK_COST)(me, rows, head)


def pick(half, me_ref, ids_ref, head_ref, mine_ref, mate_ref, rows):
    ids = ids_ref[256 * half : 256 * half + 256, :]
    for j in range(WIDTH // 128):
        rows[:, 128 * j : 128 * j + 128] = jnp.where(hits_of(me_ref[0], ids, j), 1.0, 0.0).astype(bf16)
    back(me_ref, rows, head_ref, mine_ref, mate_ref)


def pick_low(*refs):
    pick(0, *refs)


def pick_high(*refs):
    pick(1, *refs)


def run_pick(kernel, me, ids, head):
    return call(kernel, "svv", [BLOCKS, BLOCKS], scratch=[pltpu.VMEM((256, WIDTH), bf16)], **BACK_COST)(me, ids, head)


def fold(*refs):
    parts, (p_keep, p_send, q_keep, q_send) = refs[:4], refs[4:]
    for zr in range(2):
        mine, got = parts[2 * zr : 2 * zr + 2]
        for zl in range(2):
            for k in range(4):
                for x in range(4):
                    total = mine[4 * zl + k, x] + got[4 * zl + k, x]
                    (p_keep if k < 2 else p_send)[x // 2, k % 2, x % 2, zr, zl] = total[:16]
                    (q_keep if x < 2 else q_send)[k // 2, k % 2, x % 2, zr, zl] = total[16:]


def run_fold(*parts):
    return call(fold, "vvvv", [("v", (2, 2, 2, 2, 2, 16, FEATURES), bf16)] * 4, moved=512 * D * 4)(*parts)


def fold_picks(*refs):
    parts, (keep, out) = refs[:4], refs[4:]
    for zr in range(2):
        mine, got = parts[2 * zr : 2 * zr + 2]
        for zl in range(2):
            for k in range(4):
                for x in range(4):
                    (keep if k < 2 else out)[k % 2, x, zr, zl] = mine[4 * zl + k, x] + got[4 * zl + k, x]


def run_fold_picks(*parts):
    return call(fold_picks, "vvvv", [("v", (2, 4, 2, 2, 32, FEATURES), bf16)] * 2, moved=512 * D * 4)(*parts)


def finish(rest_ref, pick_ref, own_ref, got_ref, out_ref):
    for start in range(0, FEATURES, 128):
        wide = min(128, FEATURES - start)
        spot = slice(start, start + wide)
        total = own_ref[:, spot].astype(f32) + got_ref[:, spot].astype(f32)
        out_ref[:, spot] = (rest_ref[:, :wide] * total[:32] + pick_ref[:, :wide] * total[32:]).astype(bf16)


def run_finish(rest, pick, own, got):
    return call(finish, "vvvv", [("v", (32, FEATURES), bf16)], moved=1 << 17)(rest, pick, own, got)[0]


def dlogits(me_ref, low_ref, high_ref, log_ref, weight_ref, ids_ref, out_ref):
    me = me_ref[0]
    for n in range(4):
        capped_ref = low_ref if n < 2 else high_ref
        rows = slice(128 * (n % 2), 128 * (n % 2) + 128)
        out_rows = slice(128 * n, 128 * n + 128)
        log_total = log_ref[out_rows, :]
        weight = weight_ref[out_rows, :]
        ids = ids_ref[out_rows, :]
        for j in range(WIDTH // 128):
            spot = slice(128 * j, 128 * j + 128)
            capped = capped_ref[rows, spot]
            prob = jnp.exp(capped - log_total)
            onehot = jnp.where(hits_of(me, ids, j), 1.0, 0.0)
            ratio = capped / softcap
            out_ref[out_rows, spot] = (weight * (prob - onehot) * (1.0 - ratio * ratio)).astype(bf16)


def run_dlogits(me, low, high, log_total, weight, ids):
    return call(
        dlogits, "svvvvv", [("v", (512, WIDTH), bf16)], flops=512 * WIDTH * 16, moved=6 * 512 * WIDTH
    )(me, low, high, log_total, weight, ids)[0]


def head_gradient(low_ref, high_ref, dlog_ref, out_ref, rows, buffer, sems):
    def copy(i):
        return pltpu.make_async_copy(buffer.at[i % 2], out_ref.at[pl.ds(512 * i, 512)], sems.at[i % 2])

    for i in range(9):
        spot = slice(512 * i, 512 * i + 512)
        rows[:256, :] = low_ref[:, spot]
        rows[256:, :] = high_ref[:, spot]
        if i >= 2:
            copy(i - 2).wait()
        buffer[i % 2] = lax.dot_general(
            rows[...], dlog_ref[...], (((0,), (0,)), ((), ())), preferred_element_type=f32
        ).astype(bf16)
        copy(i).start()
    copy(7).wait()
    copy(8).wait()


def run_head_gradient(low, high, dlog):
    return call(
        head_gradient,
        "vvv",
        [("h", (D, WIDTH), bf16)],
        scratch=[
            pltpu.VMEM((512, 512), bf16),
            pltpu.VMEM((2, 512, WIDTH), bf16),
            pltpu.SemaphoreType.DMA((2,)),
        ],
        flops=2 * 512 * WIDTH * D,
        moved=2 * D * WIDTH,
    )(low, high, dlog)[0]


def tie(*arrays):
    return lax.optimization_barrier(arrays)


def add(a, b):
    return (a.astype(f32) + b.astype(f32)).astype(bf16)


def halve(keep, got):
    n = keep.shape[0] // 2
    return add(keep[:n], got[:n]), add(keep[n:], got[n:])


def local(hidden, head, verdict_ids, row_weight):
    me = (lax.axis_index("dp") * 8 + lax.axis_index("vocab")).astype(jnp.int32).reshape(1)
    ids, weight = run_spread(me, verdict_ids.astype(f32).reshape(4, 128), row_weight.reshape(4, 128))

    a1, a2 = send(hidden, X1), send(hidden, X2)
    o0 = send(hidden, ZH)

    g0_mine, g0_mate = run_pick(pick_low, me, ids, head)
    a1, g0_mine = tie(a1, g0_mine)
    a3 = send(a1, X2)
    o1, o2, o3 = send(o0, X1), send(o0, X2), send(a3, ZH)
    g1_mine, g1_mate = run_pick(pick_high, me, ids, head)
    g_keep, g_send = run_fold_picks(g0_mine, send(g0_mate, CORE), g1_mine, send(g1_mate, CORE))
    g_got = send(g_send, Y2)

    own_half = [hidden, a1, a2, a3]
    own_half += [send(piece, CORE) for piece in own_half]
    rows0, capped0, term0, total0, target0 = run_forward(forward_low, me, own_half, ids, head)
    a0_mine, a0_mate = run_back(me, term0, head)
    o3, total0, a0_mate = tie(o3, total0, a0_mate)
    other_half = [o0, o1, o2, o3]
    other_half += [send(piece, CORE) for piece in other_half]
    rows1, capped1, term1, total1, target1 = run_forward(forward_high, me, other_half, ids, head)
    a1_mine, a1_mate = run_back(me, term1, head)
    p_keep, p_send, q_keep, q_send = run_fold(a0_mine, send(a0_mate, CORE), a1_mine, send(a1_mate, CORE))

    total0, p_keep = tie(total0, p_keep)
    arrived = lax.all_to_all(run_pack(me, total0, total1, target0, target1), AXES, 0, 0, tiled=True)
    log_total, own, rest, pick = run_unpack(me, arrived, weight)
    dlog = run_dlogits(me, capped0, capped1, log_total, weight, ids)
    head_grad = run_head_gradient(rows0, rows1, dlog)

    p_got, q_got = send(p_send, Y2), send(q_send, X2)
    p_keep, p_send = halve(p_keep, p_got)
    q_keep, q_send = halve(q_keep, q_got)
    g_keep, g_send = halve(g_keep, g_got)
    p_got, q_got, g_got = send(p_send, X2), send(q_send, Y2), send(g_send, Y1)
    both_keep, both_send = (
        jnp.concatenate([add(p_keep[0, i], p_got[0, i]), add(q_keep[0, i], q_got[0, i])], axis=3) for i in (0, 1)
    )
    g_keep, g_send = halve(g_keep[0], g_got[0])
    both_keep, both_send = halve(both_keep, send(both_send, Y1))
    g_keep, g_send = halve(g_keep, send(g_send, X2))
    both = add(both_keep[0], send(both_send[0], X1))
    g = add(g_keep[0], send(g_send[0], X1))
    both = jnp.concatenate([both, g], axis=2)
    got = send(both[1], ZH)
    keep, out = add(both[0, 0], got[1]), add(both[0, 1], got[0])
    hidden_grad = run_finish(rest, pick, keep, send(out, ZL))
    return (own[:, 0], head_grad, hidden_grad)


def solution(mesh):
    in_specs = (P("dp", None), P(None, ("dp", "vocab")), P(), P())
    out_specs = (P("dp"), P(None, ("dp", "vocab")), P("dp", "vocab"))
    return jax.shard_map(local, mesh=mesh, in_specs=in_specs, out_specs=out_specs, check_vma=False)
```

```python
import jax
import jax.numpy as jnp
from jax import lax
from jax.experimental import pallas as pl
from jax.experimental.pallas import tpu as pltpu
from jax.sharding import PartitionSpec as P

softcap = 30.0
AXES = ("dp", "vocab")
bf16 = jnp.bfloat16
f32 = jnp.float32
D = 4608
WIDTH = 1024
FEATURES = 576
COLUMN = (512, 128)


def flips(core0, core1):
    return [(i, i ^ (core1 if i & 8 else core0)) for i in range(128)]


CORE = flips(8, 8)
X1, X2 = flips(16, 48), flips(48, 16)
Y1, Y2 = flips(1, 3), flips(3, 1)
X3, Y3 = flips(32, 32), flips(2, 2)
ZL, Z2, ZH = flips(4, 4), flips(64, 64), flips(68, 68)


def send(array, partner):
    return lax.ppermute(array, AXES, partner)


def slot_flip(slot, core):
    return (0, 1 + 2 * core, 3 - 2 * core, 2)[slot]


def whole_block(me, i):
    core = ((me >> 3) & 1) ^ ((i >> 2) & 1)
    x = ((me >> 4) & 3) ^ slot_flip(i & 3, core)
    return ((me >> 6) ^ (i >> 3)) * 8 + x * 2 + core


def feature_slot(me, i, other):
    core = ((me >> 3) & 1) ^ other
    apart = (me & 3) ^ (i & 3)
    slot = jnp.where(apart == 1 + 2 * core, 1, jnp.where(apart == 3 - 2 * core, 2, jnp.where(apart == 2, 3, 0)))
    return (((me >> 2) & 1) ^ (i >> 2)) * 4 + slot


def call(kernel, ins, outs, scratch=(), flops=0, moved=0, mib=16, aliases={}):
    places = {"v": pltpu.VMEM, "s": pltpu.SMEM, "h": pl.ANY}
    return pl.pallas_call(
        kernel,
        in_specs=[pl.BlockSpec(memory_space=places[i]) for i in ins],
        out_specs=[pl.BlockSpec(memory_space=places[o[0]]) for o in outs],
        out_shape=[jax.ShapeDtypeStruct(o[1], o[2]) for o in outs],
        scratch_shapes=list(scratch),
        input_output_aliases=aliases,
        compiler_params=pltpu.CompilerParams(vmem_limit_bytes=mib << 20),
        cost_estimate=pl.CostEstimate(flops=flops, bytes_accessed=moved, transcendentals=0),
        name=kernel.__name__,
    )


def rows_of(i):
    return slice(32 * i, 32 * i + 32)


def from_lanes(row):
    return jnp.broadcast_to(row, (128, 128)).T


def local_block(me, i, whole):
    return whole[pl.ds(pl.multiple_of(whole_block(me, i) * 32, 32), 32), :]


def hits_of(me, ids, j):
    lane = lax.broadcasted_iota(jnp.int32, (ids.shape[0], 128), 1)
    return ids == (lane + (me * WIDTH + 128 * j)).astype(f32)


def forward(half, me_ref, *refs):
    pieces, (ids_ref, head_ref, rows, capped_ref, term_ref, total_ref, target_ref) = refs[:8], refs[8:]
    me = me_ref[0]
    for i in range(8):
        rows[rows_of(i), :] = pieces[i][...]
    ids = ids_ref[256 * half : 256 * half + 256, :]
    total = jnp.zeros((256, 128), f32)
    target = jnp.zeros((256, 128), f32)
    for n in range(4):
        raw = jnp.dot(rows[...], head_ref[:, 256 * n : 256 * n + 256], preferred_element_type=f32)
        ratio = jnp.tanh(raw / softcap)
        for j in range(2):
            start = 256 * n + 128 * j
            part = ratio[:, 128 * j : 128 * j + 128]
            capped = softcap * part
            expo = jnp.exp(capped)
            hit = hits_of(me, ids, 2 * n + j)
            capped_ref[:, start : start + 128] = capped
            term_ref[:, start : start + 128] = jnp.where(hit, 0.0, expo * (1.0 - part * part)).astype(bf16)
            total = total + expo
            target = target + jnp.where(hit, capped, 0.0)
    total_ref[...] = total
    target_ref[...] = target


def forward_low(*refs):
    forward(0, *refs)


def forward_high(*refs):
    forward(1, *refs)


def run_forward(kernel, me, pieces, ids, head):
    return call(
        kernel,
        "s" + "v" * 10,
        [
            ("v", (256, D), bf16),
            ("v", (256, WIDTH), f32),
            ("v", (256, WIDTH), bf16),
            ("v", (256, 128), f32),
            ("v", (256, 128), f32),
        ],
        flops=2 * 256 * D * WIDTH,
        moved=2 * D * WIDTH,
    )(me, *pieces, ids, head)


def pack(me_ref, total0, total1, target0, target1, out_ref, whole):
    me = me_ref[0]
    sums = []
    for halves in ((total0, total1), (target0, target1)):
        for i in range(16):
            spot = pl.ds(pl.multiple_of(whole_block(me, i) * 32, 32), 32)
            whole[spot, :] = halves[i // 8][rows_of(i % 8), :]
        for j in range(4):
            sums.append(jnp.sum(whole[128 * j : 128 * j + 128, :].T, axis=0, keepdims=True))
    out_ref[...] = jnp.concatenate(sums, axis=0)


def run_pack(me, *columns):
    return call(pack, "svvvv", [("v", (8, 128), f32)], scratch=[pltpu.VMEM(COLUMN, f32)], moved=1 << 20)(
        me, *columns
    )[0]


def unpack(me_ref, sums_ref, weight_ref, log_ref, own_ref, rest_ref, pick_ref, logs, targets):
    me = me_ref[0]
    sums = sums_ref[...]
    for j in range(4):
        logs[128 * j : 128 * j + 128, :] = from_lanes(jnp.log(sums[j : j + 1, :]))
        targets[128 * j : 128 * j + 128, :] = from_lanes(sums[4 + j : 5 + j, :])
    for i in range(16):
        log_ref[rows_of(i), :] = local_block(me, i, logs)
    own_ref[...] = local_block(me, 0, targets) - local_block(me, 0, logs)
    for zr in range(2):
        for x in range(4):
            i = 8 * zr + x
            log_total = log_ref[rows_of(i), :]
            target = local_block(me, i, targets)
            weight = weight_ref[rows_of(i), :]
            ratio = target / softcap
            rest_ref[rows_of(4 * zr + x), :] = weight * jnp.exp(-log_total)
            pick_ref[rows_of(4 * zr + x), :] = weight * (jnp.exp(target - log_total) - 1.0) * (1.0 - ratio * ratio)


def run_unpack(me, sums, weight):
    outs = [("v", COLUMN, f32), ("v", (32, 128), f32), ("v", (256, 128), f32), ("v", (256, 128), f32)]
    return call(unpack, "svv", outs, scratch=[pltpu.VMEM(COLUMN, f32)] * 2, moved=1 << 20)(me, sums, weight)


def back_part(me, n, rows, head_ref, mine_ref, mate_ref):
    out = lax.dot_general(
        rows, head_ref[1152 * n : 1152 * n + 1152, :], (((1,), (1,)), ((), ())), preferred_element_type=f32
    ).astype(bf16)
    for i in range(2):
        part = out[:, FEATURES * i : FEATURES * i + FEATURES]
        mine_ref[feature_slot(me, 2 * n + i, 0)] = part[:128].reshape(4, 32, FEATURES)
        mate_ref[feature_slot(me, 2 * n + i, 1)] = part[128:].reshape(4, 32, FEATURES)


def back(me_ref, rows_ref, head_ref, mine_ref, mate_ref):
    for n in range(4):
        back_part(me_ref[0], n, rows_ref[...], head_ref, mine_ref, mate_ref)


BLOCKS = ("v", (8, 4, 32, FEATURES), bf16)
BACK_COST = dict(flops=2 * 256 * D * WIDTH, moved=2 * D * WIDTH)


def run_back(me, rows, head):
    return call(back, "svv", [BLOCKS, BLOCKS], **BACK_COST)(me, rows, head)


def begin(me_ref, ids_ref, weight_ref, head_ref, mine0, mate0, mine1, mate1, held_ref, ids_out, weight_out, *scratch):
    ids_near, weight_near, ids_whole, weight_whole, rows, sems = scratch
    me = me_ref[0]
    small = [
        pltpu.make_async_copy(ids_ref, ids_near, sems.at[4]),
        pltpu.make_async_copy(weight_ref, weight_near, sems.at[5]),
    ]
    loads = []
    for n in range(4):
        spot = pl.ds(1152 * n, 1152)
        loads.append(pltpu.make_async_copy(head_ref.at[spot], held_ref.at[spot], sems.at[n]))
    for copy in small + loads:
        copy.start()
    for copy in small:
        copy.wait()
    for j in range(4):
        ids_whole[128 * j : 128 * j + 128, :] = from_lanes(ids_near[j : j + 1, :].astype(f32))
        weight_whole[128 * j : 128 * j + 128, :] = from_lanes(weight_near[j : j + 1, :])
    for i in range(16):
        ids_out[rows_of(i), :] = local_block(me, i, ids_whole)
        weight_out[rows_of(i), :] = local_block(me, i, weight_whole)
    ids = ids_out[...]
    for j in range(WIDTH // 128):
        rows[:, 128 * j : 128 * j + 128] = jnp.where(hits_of(me, ids, j), 1.0, 0.0).astype(bf16)
    for n in range(4):
        loads[n].wait()
        for half, (mine, mate) in enumerate(((mine0, mate0), (mine1, mate1))):
            back_part(me, n, rows[256 * half : 256 * half + 256, :], held_ref, mine, mate)


def run_begin(me, ids, weight, head):
    column = ("v", COLUMN, f32)
    return call(
        begin,
        "shhh",
        [BLOCKS] * 4 + [("v", (D, WIDTH), bf16), column, column],
        scratch=[
            pltpu.VMEM((4, 128), jnp.int32),
            pltpu.VMEM((4, 128), f32),
            pltpu.VMEM(COLUMN, f32),
            pltpu.VMEM(COLUMN, f32),
            pltpu.VMEM((512, WIDTH), bf16),
            pltpu.SemaphoreType.DMA((6,)),
        ],
        flops=4 * 256 * D * WIDTH,
        moved=2 * D * WIDTH,
    )(me, *(pltpu.with_memory_space_constraint(array, pltpu.HBM) for array in (ids, weight, head)))


def fold(*refs):
    parts, (p_keep, p_send, q_keep, q_send) = refs[:4], refs[4:]
    for zr in range(2):
        mine, got = parts[2 * zr : 2 * zr + 2]
        for zl in range(2):
            for k in range(4):
                for x in range(4):
                    total = mine[4 * zl + k, x] + got[4 * zl + k, x]
                    (p_keep if k < 2 else p_send)[x // 2, k % 2, x % 2, zr, zl] = total[:16]
                    (q_keep if x < 2 else q_send)[k // 2, k % 2, x % 2, zr, zl] = total[16:]


def run_fold(*parts):
    return call(fold, "vvvv", [("v", (2, 2, 2, 2, 2, 16, FEATURES), bf16)] * 4, moved=512 * D * 4)(*parts)


def combine(first_row, slots, rest_ref, pick_ref, a_ref, a_got, g_ref, g_got, keep, out):
    for h in range(2):
        for i in range(2):
            for j in range(2):
                x = slots(h, j)
                for zr in range(2):
                    start_row = 128 * zr + 32 * x + first_row
                    rest = rest_ref[start_row : start_row + 16, :]
                    pick = pick_ref[start_row : start_row + 16, :]
                    for zl in range(2):
                        for start in range(0, FEATURES, 128):
                            wide = min(128, FEATURES - start)
                            at = (h, i, j, zr, zl, slice(None), slice(start, start + wide))
                            terms = (a_ref[at] + a_got[at]).astype(f32)
                            columns = (g_ref[at] + g_got[at]).astype(f32)
                            total = rest[:, :wide] * terms + pick[:, :wide] * columns
                            (out if h else keep)[at[1:]] = total.astype(bf16)


def combine_p(*refs):
    combine(0, lambda h, j: 2 * h + j, *refs)


def combine_q(*refs):
    combine(16, lambda h, j: j, *refs)


def run_combine(kernel, rest, pick, *parts):
    half = ("v", (2, 2, 2, 2, 16, FEATURES), bf16)
    return call(kernel, "v" * 6, [half, half], moved=1 << 22)(rest, pick, *parts)


def finish(*refs):
    terms, out_ref = refs[:4], refs[4]
    out_ref[...] = sum(term[...].astype(f32) for term in terms).astype(bf16)


def run_finish(*terms):
    return call(finish, "v" * 4, [("v", (32, FEATURES), bf16)], moved=1 << 17)(*terms)[0]


def dlogits(me_ref, low_ref, high_ref, log_ref, weight_ref, ids_ref, out_ref):
    me = me_ref[0]
    for n in range(4):
        capped_ref = low_ref if n < 2 else high_ref
        rows = slice(128 * (n % 2), 128 * (n % 2) + 128)
        out_rows = slice(128 * n, 128 * n + 128)
        log_total = log_ref[out_rows, :]
        weight = weight_ref[out_rows, :]
        ids = ids_ref[out_rows, :]
        for j in range(WIDTH // 128):
            spot = slice(128 * j, 128 * j + 128)
            capped = capped_ref[rows, spot]
            prob = jnp.exp(capped - log_total)
            onehot = jnp.where(hits_of(me, ids, j), 1.0, 0.0)
            ratio = capped / softcap
            out_ref[out_rows, spot] = (weight * (prob - onehot) * (1.0 - ratio * ratio)).astype(bf16)


def run_dlogits(me, low, high, log_total, weight, ids):
    return call(
        dlogits, "svvvvv", [("v", (512, WIDTH), bf16)], flops=512 * WIDTH * 16, moved=6 * 512 * WIDTH
    )(me, low, high, log_total, weight, ids)[0]


def head_rows(first, last, low_ref, high_ref, dlog_ref, out_ref, rows, buffer, sems):
    def copy(i):
        return pltpu.make_async_copy(buffer.at[i % 2], out_ref.at[pl.ds(512 * i, 512)], sems.at[i % 2])

    for i in range(first, last):
        spot = slice(512 * i, 512 * i + 512)
        rows[:256, :] = low_ref[:, spot]
        rows[256:, :] = high_ref[:, spot]
        if i >= first + 2:
            copy(i - 2).wait()
        buffer[i % 2] = lax.dot_general(
            rows[...], dlog_ref[...], (((0,), (0,)), ((), ())), preferred_element_type=f32
        ).astype(bf16)
        copy(i).start()
    copy(last - 2).wait()
    copy(last - 1).wait()


def head_gradient_low(low_ref, high_ref, dlog_ref, out_ref, *scratch):
    head_rows(0, 5, low_ref, high_ref, dlog_ref, out_ref, *scratch)


def head_gradient_high(low_ref, high_ref, dlog_ref, started_ref, out_ref, *scratch):
    head_rows(5, 9, low_ref, high_ref, dlog_ref, out_ref, *scratch)


def run_head_gradient(kernel, low, high, dlog, started=()):
    return call(
        kernel,
        "vvv" + "h" * len(started),
        [("h", (D, WIDTH), bf16)],
        scratch=[
            pltpu.VMEM((512, 512), bf16),
            pltpu.VMEM((2, 512, WIDTH), bf16),
            pltpu.SemaphoreType.DMA((2,)),
        ],
        flops=512 * WIDTH * D,
        moved=D * WIDTH,
        aliases={3: 0} if started else {},
    )(low, high, dlog, *started)[0]


def tie(*arrays):
    return lax.optimization_barrier(arrays)


def halve(keep_ref, got_ref, keep, out):
    n = keep.shape[0]
    keep[...] = keep_ref[:n] + got_ref[:n]
    out[...] = keep_ref[n:] + got_ref[n:]


def run_halve(held, got):
    n = held.shape[0] // 2
    half = ("v", (n,) + held.shape[1:], bf16)
    return call(halve, "vv", [half, half], moved=held.size * 6)(held, got)


def join(p_keep, p_got, q_keep, q_got, keep, out):
    for k, target in enumerate((keep, out)):
        target[:, :, :, :16] = p_keep[k] + p_got[k]
        target[:, :, :, 16:] = q_keep[k] + q_got[k]


def run_join(*parts):
    half = ("v", (2, 2, 2, 32, FEATURES), bf16)
    return call(join, "v" * 4, [half, half], moved=1 << 22)(*parts)


def split(keep, got, *outs):
    for z, out in enumerate(outs):
        out[...] = keep[0, z // 2, z % 2] + got[0, z // 2, z % 2]


def run_split(*parts):
    return call(split, "vv", [("v", (32, FEATURES), bf16)] * 4, moved=1 << 20)(*parts)


def local(hidden, head, verdict_ids, row_weight):
    me = (lax.axis_index("dp") * 8 + lax.axis_index("vocab")).astype(jnp.int32).reshape(1)
    a1, a2, a3 = send(hidden, X1), send(hidden, X2), send(hidden, X3)
    o0 = send(hidden, ZH)
    g0_mine, g0_mate, g1_mine, g1_mate, head, ids, weight = run_begin(
        me, verdict_ids.reshape(4, 128), row_weight.reshape(4, 128), head
    )
    a1, a2, a3, o0, g0_mine, g0_mate, g1_mine, g1_mate = tie(a1, a2, a3, o0, g0_mine, g0_mate, g1_mine, g1_mate)
    o1, o2, o3 = send(o0, X1), send(o0, X2), send(a3, ZH)
    g0_got, g1_got = send(g0_mate, CORE), send(g1_mate, CORE)
    gp_keep, gp_send, gq_keep, gq_send = run_fold(g0_mine, g0_got, g1_mine, g1_got)
    o1, gp_send, gq_send, a1 = tie(o1, gp_send, gq_send, a1)
    gp_got, gq_got = send(gp_send, Y2), send(gq_send, X2)
    own_half = [hidden, a1, a2, a3]
    own_half += [send(piece, CORE) for piece in own_half]
    rows0, capped0, term0, total0, target0 = run_forward(forward_low, me, own_half, ids, head)
    a0_mine, a0_mate = run_back(me, term0, head)
    o1, o2, o3, gp_got, gq_got, a0_mate = tie(o1, o2, o3, gp_got, gq_got, a0_mate)
    other_half = [o0, o1, o2, o3]
    other_half += [send(piece, CORE) for piece in other_half]
    rows1, capped1, term1, total1, target1 = run_forward(forward_high, me, other_half, ids, head)

    def step(sums, *partners):
        got = tie(*(send(sums, partner) for partner in partners))
        return sums + sum(got)

    sums = step(run_pack(me, total0, total1, target0, target1), X1)
    a1_mine, a1_mate = run_back(me, term1, head)
    sums, a1_mate = tie(sums, a1_mate)
    a1_got = send(a1_mate, CORE)
    sums = step(sums, X2)
    sums, a1_got = tie(sums, a1_got)
    p_keep, p_send, q_keep, q_send = run_fold(a0_mine, send(a0_mate, CORE), a1_mine, a1_got)

    p_got, q_got = send(p_send, Y2), send(q_send, X2)
    sums = step(step(step(sums, CORE), ZL, Z2, ZH), Y1, Y2, Y3)
    sums, p_got, q_got = tie(sums, p_got, q_got)
    log_total, own, rest, pick = run_unpack(me, sums, weight)
    p_keep, p_send = run_combine(combine_p, rest, pick, p_keep, p_got, gp_keep, gp_got)
    q_keep, q_send = run_combine(combine_q, rest, pick, q_keep, q_got, gq_keep, gq_got)
    p_got, q_got = send(p_send, X2), send(q_send, Y2)
    log_total, p_keep = tie(log_total, p_keep)
    dlog = run_dlogits(me, capped0, capped1, log_total, weight, ids)
    head_grad = run_head_gradient(head_gradient_low, rows0, rows1, dlog)
    p_got, q_got, head_grad = tie(p_got, q_got, head_grad)
    keep, out = run_join(p_keep, p_got, q_keep, q_got)
    got = send(out, Y1)
    head_grad = run_head_gradient(head_gradient_high, rows0, rows1, dlog, (head_grad,))
    got, head_grad = tie(got, head_grad)
    keep, out = run_halve(keep, got)
    keep, *outs = run_split(keep, send(out, X1))
    z_got = tie(*(send(out, partner) for out, partner in zip(outs, (ZL, Z2, ZH))))
    hidden_grad = run_finish(keep, *z_got)
    return (own[:, 0], head_grad, hidden_grad)


def solution(mesh):
    in_specs = (P("dp", None), P(None, ("dp", "vocab")), P(), P())
    out_specs = (P("dp"), P(None, ("dp", "vocab")), P("dp", "vocab"))
    return jax.shard_map(local, mesh=mesh, in_specs=in_specs, out_specs=out_specs, check_vma=False)
```

```python
import jax
import jax.numpy as jnp
from jax import lax
from jax.experimental import pallas as pl
from jax.experimental.pallas import tpu as pltpu
from jax.sharding import PartitionSpec as P

softcap = 30.0
AXES = ("dp", "vocab")
bf16 = jnp.bfloat16
f32 = jnp.float32
D = 4608
WIDTH = 1024
FEATURES = 576
COLUMN = (512, 128)


def flips(core0, core1):
    return [(i, i ^ (core1 if i & 8 else core0)) for i in range(128)]


CORE = flips(8, 8)
XY1 = flips(16 ^ 1, 48 ^ 3)
X1, X2 = flips(16, 48), flips(48, 16)
Y1, Y2 = flips(1, 3), flips(3, 1)
X3, Y3 = flips(32, 32), flips(2, 2)
ZL, Z2, ZH = flips(4, 4), flips(64, 64), flips(68, 68)


def send(array, partner):
    return lax.ppermute(array, AXES, partner)


def slot_flip(slot, core):
    return (0, 1 + 2 * core, 3 - 2 * core, 2)[slot]


def whole_block(me, i):
    core = ((me >> 3) & 1) ^ ((i >> 2) & 1)
    x = ((me >> 4) & 3) ^ slot_flip(i & 3, core)
    return ((me >> 6) ^ (i >> 3)) * 8 + x * 2 + core


def feature_slot(me, i, other):
    core = ((me >> 3) & 1) ^ other
    apart = (me & 3) ^ (i & 3)
    slot = jnp.where(apart == 1 + 2 * core, 1, jnp.where(apart == 3 - 2 * core, 2, jnp.where(apart == 2, 3, 0)))
    return (((me >> 2) & 1) ^ (i >> 2)) * 4 + slot


def call(kernel, ins, outs, scratch=(), flops=0, moved=0, mib=16, aliases={}):
    places = {"v": pltpu.VMEM, "s": pltpu.SMEM, "h": pl.ANY}
    return pl.pallas_call(
        kernel,
        in_specs=[pl.BlockSpec(memory_space=places[i]) for i in ins],
        out_specs=[pl.BlockSpec(memory_space=places[o[0]]) for o in outs],
        out_shape=[jax.ShapeDtypeStruct(o[1], o[2]) for o in outs],
        scratch_shapes=list(scratch),
        input_output_aliases=aliases,
        compiler_params=pltpu.CompilerParams(vmem_limit_bytes=mib << 20),
        cost_estimate=pl.CostEstimate(flops=flops, bytes_accessed=moved, transcendentals=0),
        name=kernel.__name__,
    )


def rows_of(i):
    return slice(32 * i, 32 * i + 32)


def from_lanes(row):
    return jnp.broadcast_to(row, (128, 128)).T


def local_block(me, i, whole):
    return whole[pl.ds(pl.multiple_of(whole_block(me, i) * 32, 32), 32), :]


def hits_of(me, ids, j):
    lane = lax.broadcasted_iota(jnp.int32, (ids.shape[0], 128), 1)
    return ids == (lane + (me * WIDTH + 128 * j)).astype(f32)


def forward(half, me_ref, *refs):
    pieces, (ids_ref, head_ref, rows, capped_ref, term_ref, total_ref, target_ref) = refs[:8], refs[8:]
    me = me_ref[0]
    for i in range(8):
        rows[rows_of(i), :] = pieces[i][...]
    ids = ids_ref[256 * half : 256 * half + 256, :]
    total = jnp.zeros((256, 128), f32)
    target = jnp.zeros((256, 128), f32)
    for n in range(4):
        raw = jnp.dot(rows[...], head_ref[:, 256 * n : 256 * n + 256], preferred_element_type=f32)
        ratio = jnp.tanh(raw / softcap)
        for j in range(2):
            start = 256 * n + 128 * j
            part = ratio[:, 128 * j : 128 * j + 128]
            capped = softcap * part
            expo = jnp.exp(capped)
            hit = hits_of(me, ids, 2 * n + j)
            capped_ref[:, start : start + 128] = capped
            term_ref[:, start : start + 128] = jnp.where(hit, 0.0, expo * (1.0 - part * part)).astype(bf16)
            total = total + expo
            target = target + jnp.where(hit, capped, 0.0)
    total_ref[...] = total
    target_ref[...] = target


def forward_low(*refs):
    forward(0, *refs)


def forward_high(*refs):
    forward(1, *refs)


def run_forward(kernel, me, pieces, ids, head):
    return call(
        kernel,
        "s" + "v" * 10,
        [
            ("v", (256, D), bf16),
            ("v", (256, WIDTH), f32),
            ("v", (256, WIDTH), bf16),
            ("v", (256, 128), f32),
            ("v", (256, 128), f32),
        ],
        flops=2 * 256 * D * WIDTH,
        moved=2 * D * WIDTH,
    )(me, *pieces, ids, head)


def pack(me_ref, total0, total1, target0, target1, out_ref, whole):
    me = me_ref[0]
    sums = []
    for halves in ((total0, total1), (target0, target1)):
        for i in range(16):
            spot = pl.ds(pl.multiple_of(whole_block(me, i) * 32, 32), 32)
            whole[spot, :] = halves[i // 8][rows_of(i % 8), :]
        for j in range(4):
            sums.append(jnp.sum(whole[128 * j : 128 * j + 128, :].T, axis=0, keepdims=True))
    out_ref[...] = jnp.concatenate(sums, axis=0)


def run_pack(me, *columns):
    return call(pack, "svvvv", [("v", (8, 128), f32)], scratch=[pltpu.VMEM(COLUMN, f32)], moved=1 << 20)(
        me, *columns
    )[0]


def unpack(me_ref, sums_ref, weight_ref, log_ref, own_ref, rest_ref, pick_ref, logs, targets):
    me = me_ref[0]
    sums = sums_ref[...]
    for j in range(4):
        logs[128 * j : 128 * j + 128, :] = from_lanes(jnp.log(sums[j : j + 1, :]))
        targets[128 * j : 128 * j + 128, :] = from_lanes(sums[4 + j : 5 + j, :])
    for i in range(16):
        log_ref[rows_of(i), :] = local_block(me, i, logs)
    own_ref[...] = local_block(me, 0, targets) - local_block(me, 0, logs)
    for zr in range(2):
        for x in range(4):
            i = 8 * zr + x
            log_total = log_ref[rows_of(i), :]
            target = local_block(me, i, targets)
            weight = weight_ref[rows_of(i), :]
            ratio = target / softcap
            rest_ref[rows_of(4 * zr + x), :] = weight * jnp.exp(-log_total)
            pick_ref[rows_of(4 * zr + x), :] = weight * (jnp.exp(target - log_total) - 1.0) * (1.0 - ratio * ratio)


def run_unpack(me, sums, weight):
    outs = [("v", COLUMN, f32), ("v", (32, 128), f32), ("v", (256, 128), f32), ("v", (256, 128), f32)]
    return call(unpack, "svv", outs, scratch=[pltpu.VMEM(COLUMN, f32)] * 2, moved=1 << 20)(me, sums, weight)


def back_part(me, n, rows, head_ref, mine_ref, mate_ref):
    out = lax.dot_general(
        rows, head_ref[1152 * n : 1152 * n + 1152, :], (((1,), (1,)), ((), ())), preferred_element_type=f32
    ).astype(bf16)
    for i in range(2):
        part = out[:, FEATURES * i : FEATURES * i + FEATURES]
        mine_ref[feature_slot(me, 2 * n + i, 0)] = part[:128].reshape(4, 32, FEATURES)
        mate_ref[feature_slot(me, 2 * n + i, 1)] = part[128:].reshape(4, 32, FEATURES)


def back(me_ref, rows_ref, head_ref, mine_ref, mate_ref):
    for n in range(4):
        back_part(me_ref[0], n, rows_ref[...], head_ref, mine_ref, mate_ref)


BLOCKS = ("v", (8, 4, 32, FEATURES), bf16)
BACK_COST = dict(flops=2 * 256 * D * WIDTH, moved=2 * D * WIDTH)


def run_back(me, rows, head):
    return call(back, "svv", [BLOCKS, BLOCKS], **BACK_COST)(me, rows, head)


def begin(me_ref, ids_ref, weight_ref, head_ref, mine0, mate0, mine1, mate1, held_ref, ids_out, weight_out, *scratch):
    ids_near, weight_near, ids_whole, weight_whole, rows, sems = scratch
    me = me_ref[0]
    small = [
        pltpu.make_async_copy(ids_ref, ids_near, sems.at[4]),
        pltpu.make_async_copy(weight_ref, weight_near, sems.at[5]),
    ]
    loads = []
    for n in range(4):
        spot = pl.ds(1152 * n, 1152)
        loads.append(pltpu.make_async_copy(head_ref.at[spot], held_ref.at[spot], sems.at[n]))
    for copy in small + loads:
        copy.start()
    for copy in small:
        copy.wait()
    for j in range(4):
        ids_whole[128 * j : 128 * j + 128, :] = from_lanes(ids_near[j : j + 1, :].astype(f32))
        weight_whole[128 * j : 128 * j + 128, :] = from_lanes(weight_near[j : j + 1, :])
    for i in range(16):
        ids_out[rows_of(i), :] = local_block(me, i, ids_whole)
        weight_out[rows_of(i), :] = local_block(me, i, weight_whole)
    ids = ids_out[...]
    for j in range(WIDTH // 128):
        rows[:, 128 * j : 128 * j + 128] = jnp.where(hits_of(me, ids, j), 1.0, 0.0).astype(bf16)
    for n in range(4):
        loads[n].wait()
        for half, (mine, mate) in enumerate(((mine0, mate0), (mine1, mate1))):
            back_part(me, n, rows[256 * half : 256 * half + 256, :], held_ref, mine, mate)


def run_begin(me, ids, weight, head):
    column = ("v", COLUMN, f32)
    return call(
        begin,
        "shhh",
        [BLOCKS] * 4 + [("v", (D, WIDTH), bf16), column, column],
        scratch=[
            pltpu.VMEM((4, 128), jnp.int32),
            pltpu.VMEM((4, 128), f32),
            pltpu.VMEM(COLUMN, f32),
            pltpu.VMEM(COLUMN, f32),
            pltpu.VMEM((512, WIDTH), bf16),
            pltpu.SemaphoreType.DMA((6,)),
        ],
        flops=4 * 256 * D * WIDTH,
        moved=2 * D * WIDTH,
    )(me, *(pltpu.with_memory_space_constraint(array, pltpu.HBM) for array in (ids, weight, head)))


def fold(*refs):
    parts, (p_keep, p_send, q_keep, q_send) = refs[:8], refs[8:]
    for zr in range(2):
        a_mine, a_got, g_mine, g_got = parts[4 * zr : 4 * zr + 4]
        for zl in range(2):
            for k in range(4):
                b = 4 * zl + k
                for x in range(4):
                    p_at = (p_keep if k < 2 else p_send).at[x // 2, k % 2, x % 2, zr, zl]
                    q_at = (q_keep if x < 2 else q_send).at[k // 2, k % 2, x % 2, zr, zl]
                    for first, mine, got in ((0, a_mine, a_got), (16, g_mine, g_got)):
                        total = mine[b, x] + got[b, x]
                        p_at[first : first + 16] = total[:16]
                        q_at[first : first + 16] = total[16:]


def run_fold(*parts):
    return call(fold, "v" * 8, [("v", (2, 2, 2, 2, 2, 32, FEATURES), bf16)] * 4, moved=512 * D * 8)(*parts)


def combine(first_row, slots, rest_ref, pick_ref, held, got, keep, out):
    for h, target in enumerate((keep, out)):
        for i in range(2):
            for j in range(2):
                x = slots(h, j)
                for zr in range(2):
                    first = 128 * zr + 32 * x + first_row
                    rest = rest_ref[first : first + 16, :]
                    pick = pick_ref[first : first + 16, :]
                    for zl in range(2):
                        for start in range(0, FEATURES, 128):
                            wide = min(128, FEATURES - start)
                            at = (h, i, j, zr, zl, slice(None), slice(start, start + wide))
                            both = (held[at] + got[at]).astype(f32)
                            total = rest[:, :wide] * both[:16] + pick[:, :wide] * both[16:]
                            target[at[1:]] = total.astype(bf16)


def combine_p(*refs):
    combine(0, lambda h, j: 2 * h + j, *refs)


def combine_q(*refs):
    combine(16, lambda h, j: j, *refs)


def run_combine(kernel, *parts):
    half = ("v", (2, 2, 2, 2, 16, FEATURES), bf16)
    return call(kernel, "v" * 4, [half, half], moved=1 << 22)(*parts)


def join(p_keep, p_got, q_keep, q_got, *outs):
    for n, out in enumerate(outs):
        out[:, :, :16] = p_keep[n // 2, n % 2] + p_got[n // 2, n % 2]
        out[:, :, 16:] = q_keep[n // 2, n % 2] + q_got[n // 2, n % 2]


def run_join(*parts):
    return call(join, "v" * 4, [("v", (2, 2, 32, FEATURES), bf16)] * 4, moved=1 << 22)(*parts)


def split(*refs):
    terms, outs = refs[:4], refs[4:]
    for z, out in enumerate(outs):
        out[...] = sum(term[z // 2, z % 2].astype(f32) for term in terms).astype(bf16)


def run_split(*parts):
    return call(split, "vvvv", [("v", (32, FEATURES), bf16)] * 4, moved=1 << 20)(*parts)


def finish(*refs):
    terms, out_ref = refs[:4], refs[4]
    out_ref[...] = sum(term[...].astype(f32) for term in terms).astype(bf16)


def run_finish(*terms):
    return call(finish, "v" * 4, [("v", (32, FEATURES), bf16)], moved=1 << 17)(*terms)[0]


def dlogits(me_ref, low_ref, high_ref, log_ref, weight_ref, ids_ref, out_ref):
    me = me_ref[0]
    for n in range(4):
        capped_ref = low_ref if n < 2 else high_ref
        rows = slice(128 * (n % 2), 128 * (n % 2) + 128)
        out_rows = slice(128 * n, 128 * n + 128)
        log_total = log_ref[out_rows, :]
        weight = weight_ref[out_rows, :]
        ids = ids_ref[out_rows, :]
        for j in range(WIDTH // 128):
            spot = slice(128 * j, 128 * j + 128)
            capped = capped_ref[rows, spot]
            prob = jnp.exp(capped - log_total)
            onehot = jnp.where(hits_of(me, ids, j), 1.0, 0.0)
            ratio = capped / softcap
            out_ref[out_rows, spot] = (weight * (prob - onehot) * (1.0 - ratio * ratio)).astype(bf16)


def run_dlogits(me, low, high, log_total, weight, ids):
    return call(
        dlogits, "svvvvv", [("v", (512, WIDTH), bf16)], flops=512 * WIDTH * 16, moved=6 * 512 * WIDTH
    )(me, low, high, log_total, weight, ids)[0]


def head_rows(first, last, low_ref, high_ref, dlog_ref, out_ref, rows, buffer, sems):
    def copy(i):
        return pltpu.make_async_copy(buffer.at[i % 2], out_ref.at[pl.ds(512 * i, 512)], sems.at[i % 2])

    for i in range(first, last):
        spot = slice(512 * i, 512 * i + 512)
        rows[:256, :] = low_ref[:, spot]
        rows[256:, :] = high_ref[:, spot]
        if i >= first + 2:
            copy(i - 2).wait()
        buffer[i % 2] = lax.dot_general(
            rows[...], dlog_ref[...], (((0,), (0,)), ((), ())), preferred_element_type=f32
        ).astype(bf16)
        copy(i).start()
    copy(last - 2).wait()
    copy(last - 1).wait()


def head_gradient_low(low_ref, high_ref, dlog_ref, out_ref, *scratch):
    head_rows(0, 5, low_ref, high_ref, dlog_ref, out_ref, *scratch)


def head_gradient_high(low_ref, high_ref, dlog_ref, started_ref, out_ref, *scratch):
    head_rows(5, 9, low_ref, high_ref, dlog_ref, out_ref, *scratch)


def run_head_gradient(kernel, low, high, dlog, started=()):
    return call(
        kernel,
        "vvv" + "h" * len(started),
        [("h", (D, WIDTH), bf16)],
        scratch=[
            pltpu.VMEM((512, 512), bf16),
            pltpu.VMEM((2, 512, WIDTH), bf16),
            pltpu.SemaphoreType.DMA((2,)),
        ],
        flops=512 * WIDTH * D,
        moved=D * WIDTH,
        aliases={3: 0} if started else {},
    )(low, high, dlog, *started)[0]


def tie(*arrays):
    return lax.optimization_barrier(arrays)


def local(hidden, head, verdict_ids, row_weight):
    me = (lax.axis_index("dp") * 8 + lax.axis_index("vocab")).astype(jnp.int32).reshape(1)
    a1, a2, a3 = send(hidden, X1), send(hidden, X2), send(hidden, X3)
    o0 = send(hidden, ZH)
    g0_mine, g0_mate, g1_mine, g1_mate, head, ids, weight = run_begin(
        me, verdict_ids.reshape(4, 128), row_weight.reshape(4, 128), head
    )
    a1, a2, a3, o0, g0_mine, g0_mate, g1_mine, g1_mate = tie(a1, a2, a3, o0, g0_mine, g0_mate, g1_mine, g1_mate)
    o1, o2, o3 = send(o0, X1), send(o0, X2), send(a3, ZH)
    g0_got, g1_got = send(g0_mate, CORE), send(g1_mate, CORE)
    own_half = [hidden, a1, a2, a3]
    own_half += [send(piece, CORE) for piece in own_half]
    rows0, capped0, term0, total0, target0 = run_forward(forward_low, me, own_half, ids, head)
    o1, term0 = tie(o1, term0)
    a0_mine, a0_mate = run_back(me, term0, head)
    o1, o2, o3, g0_got, g1_got, a0_mate = tie(o1, o2, o3, g0_got, g1_got, a0_mate)
    other_half = [o0, o1, o2, o3]
    other_half += [send(piece, CORE) for piece in other_half]
    rows1, capped1, term1, total1, target1 = run_forward(forward_high, me, other_half, ids, head)

    def step(sums, *partners):
        got = tie(*(send(sums, partner) for partner in partners))
        return sums + sum(got)

    sums = step(run_pack(me, total0, total1, target0, target1), X1)
    a1_mine, a1_mate = run_back(me, term1, head)
    sums, a1_mate = tie(sums, a1_mate)
    a1_got = send(a1_mate, CORE)
    sums = step(sums, X2)
    sums, a1_got = tie(sums, a1_got)
    p_keep, p_send, q_keep, q_send = run_fold(
        a0_mine, send(a0_mate, CORE), g0_mine, g0_got, a1_mine, a1_got, g1_mine, g1_got
    )

    p_got, q_got = send(p_send, Y2), send(q_send, X2)
    sums = step(step(step(sums, CORE), ZL, Z2, ZH), Y1, Y2, Y3)
    sums, p_got, q_got = tie(sums, p_got, q_got)
    log_total, own, rest, pick = run_unpack(me, sums, weight)
    p_keep, p_send = run_combine(combine_p, rest, pick, p_keep, p_got)
    q_keep, q_send = run_combine(combine_q, rest, pick, q_keep, q_got)
    p_got, q_got = send(p_send, X2), send(q_send, Y2)
    log_total, p_keep = tie(log_total, p_keep)
    dlog = run_dlogits(me, capped0, capped1, log_total, weight, ids)
    head_grad = run_head_gradient(head_gradient_low, rows0, rows1, dlog)
    p_got, q_got, head_grad = tie(p_got, q_got, head_grad)
    keep, *outs = run_join(p_keep, p_got, q_keep, q_got)
    got = [send(out, partner) for out, partner in zip(outs, (X1, Y1, XY1))]
    head_grad = run_head_gradient(head_gradient_high, rows0, rows1, dlog, (head_grad,))
    *got, head_grad = tie(*got, head_grad)
    keep, *outs = run_split(keep, *got)
    z_got = tie(*(send(out, partner) for out, partner in zip(outs, (ZL, Z2, ZH))))
    hidden_grad = run_finish(keep, *z_got)
    return (own[:, 0], head_grad, hidden_grad)


def solution(mesh):
    in_specs = (P("dp", None), P(None, ("dp", "vocab")), P(), P())
    out_specs = (P("dp"), P(None, ("dp", "vocab")), P("dp", "vocab"))
    return jax.shard_map(local, mesh=mesh, in_specs=in_specs, out_specs=out_specs, check_vma=False)
```

```python
import jax
import jax.numpy as jnp
from jax import lax
from jax.experimental import pallas as pl
from jax.experimental.pallas import tpu as pltpu
from jax.sharding import PartitionSpec as P

softcap = 30.0
AXES = ("dp", "vocab")
bf16 = jnp.bfloat16
f32 = jnp.float32
D = 4608
WIDTH = 1024
FEATURES = 576
COLUMN = (512, 128)


def flips(core0, core1):
    return [(i, i ^ (core1 if i & 8 else core0)) for i in range(128)]


CORE = flips(8, 8)
XY1 = flips(16 ^ 1, 48 ^ 3)
X1, X2 = flips(16, 48), flips(48, 16)
Y1, Y2 = flips(1, 3), flips(3, 1)
X3, Y3 = flips(32, 32), flips(2, 2)
ZL, Z2, ZH = flips(4, 4), flips(64, 64), flips(68, 68)


def send(array, partner):
    return lax.ppermute(array, AXES, partner)


def slot_flip(slot, core):
    return (0, 1 + 2 * core, 3 - 2 * core, 2)[slot]


def whole_block(me, i):
    core = ((me >> 3) & 1) ^ ((i >> 2) & 1)
    x = ((me >> 4) & 3) ^ slot_flip(i & 3, core)
    return ((me >> 6) ^ (i >> 3)) * 8 + x * 2 + core


def feature_slot(me, i, other):
    core = ((me >> 3) & 1) ^ other
    apart = (me & 3) ^ (i & 3)
    return jnp.where(apart == 1 + 2 * core, 1, jnp.where(apart == 3 - 2 * core, 2, jnp.where(apart == 2, 3, 0)))


def call(kernel, ins, outs, scratch=(), flops=0, moved=0, mib=16, aliases={}):
    places = {"v": pltpu.VMEM, "s": pltpu.SMEM, "h": pl.ANY}
    return pl.pallas_call(
        kernel,
        in_specs=[pl.BlockSpec(memory_space=places[i]) for i in ins],
        out_specs=[pl.BlockSpec(memory_space=places[o[0]]) for o in outs],
        out_shape=[jax.ShapeDtypeStruct(o[1], o[2]) for o in outs],
        scratch_shapes=list(scratch),
        input_output_aliases=aliases,
        compiler_params=pltpu.CompilerParams(vmem_limit_bytes=mib << 20),
        cost_estimate=pl.CostEstimate(flops=flops, bytes_accessed=moved, transcendentals=0),
        name=kernel.__name__,
    )


def rows_of(i):
    return slice(32 * i, 32 * i + 32)


def from_lanes(row):
    return jnp.broadcast_to(row, (128, 128)).T


def local_block(me, i, whole):
    return whole[pl.ds(pl.multiple_of(whole_block(me, i) * 32, 32), 32), :]


def hits_of(me, ids, j):
    lane = lax.broadcasted_iota(jnp.int32, (ids.shape[0], 128), 1)
    return ids == (lane + (me * WIDTH + 128 * j)).astype(f32)


def forward(half, me_ref, *refs):
    pieces, (ids_ref, head_ref, rows, capped_ref, term_ref, total_ref, target_ref) = refs[:8], refs[8:]
    me = me_ref[0]
    for i in range(8):
        rows[rows_of(i), :] = pieces[i][...]
    ids = ids_ref[256 * half : 256 * half + 256, :]
    total = jnp.zeros((256, 128), f32)
    target = jnp.zeros((256, 128), f32)
    for n in range(4):
        raw = jnp.dot(rows[...], head_ref[:, 256 * n : 256 * n + 256], preferred_element_type=f32)
        ratio = jnp.tanh(raw / softcap)
        for j in range(2):
            start = 256 * n + 128 * j
            part = ratio[:, 128 * j : 128 * j + 128]
            capped = softcap * part
            expo = jnp.exp(capped)
            hit = hits_of(me, ids, 2 * n + j)
            capped_ref[:, start : start + 128] = capped
            term_ref[:, start : start + 128] = jnp.where(hit, 0.0, expo * (1.0 - part * part)).astype(bf16)
            total = total + expo
            target = target + jnp.where(hit, capped, 0.0)
    total_ref[...] = total
    target_ref[...] = target


def forward_low(*refs):
    forward(0, *refs)


def forward_high(*refs):
    forward(1, *refs)


def run_forward(kernel, me, pieces, ids, head):
    return call(
        kernel,
        "s" + "v" * 10,
        [
            ("v", (256, D), bf16),
            ("v", (256, WIDTH), f32),
            ("v", (256, WIDTH), bf16),
            ("v", (256, 128), f32),
            ("v", (256, 128), f32),
        ],
        flops=2 * 256 * D * WIDTH,
        moved=2 * D * WIDTH,
    )(me, *pieces, ids, head)


def pack(me_ref, total0, total1, target0, target1, out_ref, whole):
    me = me_ref[0]
    sums = []
    for halves in ((total0, total1), (target0, target1)):
        for i in range(16):
            spot = pl.ds(pl.multiple_of(whole_block(me, i) * 32, 32), 32)
            whole[spot, :] = halves[i // 8][rows_of(i % 8), :]
        for j in range(4):
            sums.append(jnp.sum(whole[128 * j : 128 * j + 128, :].T, axis=0, keepdims=True))
    out_ref[...] = jnp.concatenate(sums, axis=0)


def run_pack(me, *columns):
    return call(pack, "svvvv", [("v", (8, 128), f32)], scratch=[pltpu.VMEM(COLUMN, f32)], moved=1 << 20)(
        me, *columns
    )[0]


def unpack(me_ref, sums_ref, weight_ref, log_ref, own_ref, rest_ref, pick_ref, logs, targets):
    me = me_ref[0]
    sums = sums_ref[...]
    for j in range(4):
        logs[128 * j : 128 * j + 128, :] = from_lanes(jnp.log(sums[j : j + 1, :]))
        targets[128 * j : 128 * j + 128, :] = from_lanes(sums[4 + j : 5 + j, :])
    for i in range(16):
        log_ref[rows_of(i), :] = local_block(me, i, logs)
    own_ref[...] = local_block(me, 0, targets) - local_block(me, 0, logs)
    for zr in range(2):
        for x in range(4):
            i = 8 * zr + x
            log_total = log_ref[rows_of(i), :]
            target = local_block(me, i, targets)
            weight = weight_ref[rows_of(i), :]
            ratio = target / softcap
            rest_ref[rows_of(4 * zr + x), :] = weight * jnp.exp(-log_total)
            pick_ref[rows_of(4 * zr + x), :] = weight * (jnp.exp(target - log_total) - 1.0) * (1.0 - ratio * ratio)


def run_unpack(me, sums, weight):
    outs = [("v", COLUMN, f32), ("v", (32, 128), f32), ("v", (256, 128), f32), ("v", (256, 128), f32)]
    return call(unpack, "svv", outs, scratch=[pltpu.VMEM(COLUMN, f32)] * 2, moved=1 << 20)(me, sums, weight)


def back_part(me, n, rows, head_ref, mine_ref, mate_ref):
    out = lax.dot_general(
        rows, head_ref[1152 * n : 1152 * n + 1152, :], (((1,), (1,)), ((), ())), preferred_element_type=f32
    ).astype(bf16)
    for i in range(2):
        part = out[:, FEATURES * i : FEATURES * i + FEATURES]
        block = 2 * n + i
        spot = slice(FEATURES * (block // 4), FEATURES * (block // 4) + FEATURES)
        mine_ref[feature_slot(me, block, 0), :, :, spot] = part[:128].reshape(4, 32, FEATURES)
        mate_ref[feature_slot(me, block, 1), :, :, spot] = part[128:].reshape(4, 32, FEATURES)


def back(me_ref, rows_ref, head_ref, mine_ref, mate_ref):
    for n in range(4):
        back_part(me_ref[0], n, rows_ref[...], head_ref, mine_ref, mate_ref)


BLOCKS = ("v", (4, 4, 32, 2 * FEATURES), bf16)
BACK_COST = dict(flops=2 * 256 * D * WIDTH, moved=2 * D * WIDTH)


def run_back(me, rows, head):
    return call(back, "svv", [BLOCKS, BLOCKS], **BACK_COST)(me, rows, head)


def begin(me_ref, ids_ref, weight_ref, head_ref, mine0, mate0, mine1, mate1, held_ref, ids_out, weight_out, *scratch):
    ids_near, weight_near, ids_whole, weight_whole, rows, sems = scratch
    me = me_ref[0]
    small = [
        pltpu.make_async_copy(ids_ref, ids_near, sems.at[4]),
        pltpu.make_async_copy(weight_ref, weight_near, sems.at[5]),
    ]
    loads = []
    for n in range(4):
        spot = pl.ds(1152 * n, 1152)
        loads.append(pltpu.make_async_copy(head_ref.at[spot], held_ref.at[spot], sems.at[n]))
    for copy in small + loads:
        copy.start()
    for copy in small:
        copy.wait()
    for j in range(4):
        ids_whole[128 * j : 128 * j + 128, :] = from_lanes(ids_near[j : j + 1, :].astype(f32))
        weight_whole[128 * j : 128 * j + 128, :] = from_lanes(weight_near[j : j + 1, :])
    for i in range(16):
        ids_out[rows_of(i), :] = local_block(me, i, ids_whole)
        weight_out[rows_of(i), :] = local_block(me, i, weight_whole)
    ids = ids_out[...]
    for j in range(WIDTH // 128):
        rows[:, 128 * j : 128 * j + 128] = jnp.where(hits_of(me, ids, j), 1.0, 0.0).astype(bf16)
    for n in range(4):
        loads[n].wait()
        for half, (mine, mate) in enumerate(((mine0, mate0), (mine1, mate1))):
            back_part(me, n, rows[256 * half : 256 * half + 256, :], held_ref, mine, mate)


def run_begin(me, ids, weight, head):
    column = ("v", COLUMN, f32)
    return call(
        begin,
        "shhh",
        [BLOCKS] * 4 + [("v", (D, WIDTH), bf16), column, column],
        scratch=[
            pltpu.VMEM((4, 128), jnp.int32),
            pltpu.VMEM((4, 128), f32),
            pltpu.VMEM(COLUMN, f32),
            pltpu.VMEM(COLUMN, f32),
            pltpu.VMEM((512, WIDTH), bf16),
            pltpu.SemaphoreType.DMA((6,)),
        ],
        flops=4 * 256 * D * WIDTH,
        moved=2 * D * WIDTH,
    )(me, *(pltpu.with_memory_space_constraint(array, pltpu.HBM) for array in (ids, weight, head)))


def fold(*refs):
    parts, (p_keep, p_send, q_keep, q_send) = refs[:8], refs[8:]
    for zr in range(2):
        a_mine, a_got, g_mine, g_got = parts[4 * zr : 4 * zr + 4]
        for k in range(4):
            for x in range(4):
                p_at = (p_keep if k < 2 else p_send).at[x // 2, k % 2, x % 2, zr]
                q_at = (q_keep if x < 2 else q_send).at[k // 2, k % 2, x % 2, zr]
                for first, mine, got in ((0, a_mine, a_got), (16, g_mine, g_got)):
                    total = mine[k, x] + got[k, x]
                    p_at[first : first + 16] = total[:16]
                    q_at[first : first + 16] = total[16:]


def run_fold(*parts):
    return call(fold, "v" * 8, [("v", (2, 2, 2, 2, 32, 2 * FEATURES), bf16)] * 4, moved=512 * D * 8)(*parts)


def combine(first_row, slots, rest_ref, pick_ref, held, got, keep, out):
    for h, target in enumerate((keep, out)):
        for i in range(2):
            for j in range(2):
                x = slots(h, j)
                for zr in range(2):
                    first = 128 * zr + 32 * x + first_row
                    rest = rest_ref[first : first + 16, :]
                    pick = pick_ref[first : first + 16, :]
                    for start in range(0, 2 * FEATURES, 128):
                        at = (h, i, j, zr, slice(None), slice(start, start + 128))
                        both = (held[at] + got[at]).astype(f32)
                        target[at[1:]] = (rest * both[:16] + pick * both[16:]).astype(bf16)


def combine_p(*refs):
    combine(0, lambda h, j: 2 * h + j, *refs)


def combine_q(*refs):
    combine(16, lambda h, j: j, *refs)


def run_combine(kernel, *parts):
    half = ("v", (2, 2, 2, 16, 2 * FEATURES), bf16)
    return call(kernel, "v" * 4, [half, half], moved=1 << 22)(*parts)


def join(p_keep, p_got, q_keep, q_got, *outs):
    for n, out in enumerate(outs):
        out[:, :16] = p_keep[n // 2, n % 2] + p_got[n // 2, n % 2]
        out[:, 16:] = q_keep[n // 2, n % 2] + q_got[n // 2, n % 2]


def run_join(*parts):
    return call(join, "v" * 4, [("v", (2, 32, 2 * FEATURES), bf16)] * 4, moved=1 << 22)(*parts)


def split(me_ref, *refs):
    terms, outs = refs[:4], refs[4:]
    low = ((me_ref[0] >> 2) & 1) == 0
    for zr in range(2):
        total = sum(term[zr].astype(f32) for term in terms)
        halves = (total[:, :FEATURES], total[:, FEATURES:])
        for zl in range(2):
            outs[2 * zr + zl][...] = jnp.where(low, halves[zl], halves[1 - zl]).astype(bf16)


def run_split(me, *parts):
    return call(split, "svvvv", [("v", (32, FEATURES), bf16)] * 4, moved=1 << 20)(me, *parts)


def finish(*refs):
    terms, out_ref = refs[:4], refs[4]
    out_ref[...] = sum(term[...].astype(f32) for term in terms).astype(bf16)


def run_finish(*terms):
    return call(finish, "v" * 4, [("v", (32, FEATURES), bf16)], moved=1 << 17)(*terms)[0]


def dlogits(me_ref, low_ref, high_ref, log_ref, weight_ref, ids_ref, out_ref):
    me = me_ref[0]
    for n in range(4):
        capped_ref = low_ref if n < 2 else high_ref
        rows = slice(128 * (n % 2), 128 * (n % 2) + 128)
        out_rows = slice(128 * n, 128 * n + 128)
        log_total = log_ref[out_rows, :]
        weight = weight_ref[out_rows, :]
        ids = ids_ref[out_rows, :]
        for j in range(WIDTH // 128):
            spot = slice(128 * j, 128 * j + 128)
            capped = capped_ref[rows, spot]
            prob = jnp.exp(capped - log_total)
            onehot = jnp.where(hits_of(me, ids, j), 1.0, 0.0)
            ratio = capped / softcap
            out_ref[out_rows, spot] = (weight * (prob - onehot) * (1.0 - ratio * ratio)).astype(bf16)


def run_dlogits(me, low, high, log_total, weight, ids):
    return call(
        dlogits, "svvvvv", [("v", (512, WIDTH), bf16)], flops=512 * WIDTH * 16, moved=6 * 512 * WIDTH
    )(me, low, high, log_total, weight, ids)[0]


def head_rows(first, last, low_ref, high_ref, dlog_ref, out_ref, rows, buffer, sems):
    def copy(i):
        return pltpu.make_async_copy(buffer.at[i % 2], out_ref.at[pl.ds(512 * i, 512)], sems.at[i % 2])

    for i in range(first, last):
        spot = slice(512 * i, 512 * i + 512)
        rows[:256, :] = low_ref[:, spot]
        rows[256:, :] = high_ref[:, spot]
        if i >= first + 2:
            copy(i - 2).wait()
        buffer[i % 2] = lax.dot_general(
            rows[...], dlog_ref[...], (((0,), (0,)), ((), ())), preferred_element_type=f32
        ).astype(bf16)
        copy(i).start()
    copy(last - 2).wait()
    copy(last - 1).wait()


def head_gradient_low(low_ref, high_ref, dlog_ref, out_ref, *scratch):
    head_rows(0, 5, low_ref, high_ref, dlog_ref, out_ref, *scratch)


def head_gradient_high(low_ref, high_ref, dlog_ref, started_ref, out_ref, *scratch):
    head_rows(5, 9, low_ref, high_ref, dlog_ref, out_ref, *scratch)


def run_head_gradient(kernel, low, high, dlog, started=()):
    return call(
        kernel,
        "vvv" + "h" * len(started),
        [("h", (D, WIDTH), bf16)],
        scratch=[
            pltpu.VMEM((512, 512), bf16),
            pltpu.VMEM((2, 512, WIDTH), bf16),
            pltpu.SemaphoreType.DMA((2,)),
        ],
        flops=512 * WIDTH * D,
        moved=D * WIDTH,
        aliases={3: 0} if started else {},
    )(low, high, dlog, *started)[0]


def tie(*arrays):
    return lax.optimization_barrier(arrays)


def local(hidden, head, verdict_ids, row_weight):
    me = (lax.axis_index("dp") * 8 + lax.axis_index("vocab")).astype(jnp.int32).reshape(1)
    a1, a2, a3 = send(hidden, X1), send(hidden, X2), send(hidden, X3)
    o0 = send(hidden, ZH)
    g0_mine, g0_mate, g1_mine, g1_mate, head, ids, weight = run_begin(
        me, verdict_ids.reshape(4, 128), row_weight.reshape(4, 128), head
    )
    a1, a2, a3, o0, g0_mine, g0_mate, g1_mine, g1_mate = tie(a1, a2, a3, o0, g0_mine, g0_mate, g1_mine, g1_mate)
    o1, o2, o3 = send(o0, X1), send(o0, X2), send(a3, ZH)
    own_half = [hidden, a1, a2, a3]
    own_half += [send(piece, CORE) for piece in own_half]
    rows0, capped0, term0, total0, target0 = run_forward(forward_low, me, own_half, ids, head)
    o1, term0 = tie(o1, term0)
    a0_mine, a0_mate = run_back(me, term0, head)
    o1, o2, o3, a0_mate = tie(o1, o2, o3, a0_mate)
    other_half = [o0, o1, o2, o3]
    *swapped, a0_mate = tie(*(send(piece, CORE) for piece in other_half), a0_mate)
    other_half += swapped
    a0_got = send(a0_mate, CORE)
    rows1, capped1, term1, total1, target1 = run_forward(forward_high, me, other_half, ids, head)

    def step(sums, *partners):
        got = tie(*(send(sums, partner) for partner in partners))
        return sums + sum(got)

    total1, a0_got, g0_mate, g1_mate = tie(total1, a0_got, g0_mate, g1_mate)
    g0_got, g1_got = send(g0_mate, CORE), send(g1_mate, CORE)
    sums = step(run_pack(me, total0, total1, target0, target1), X1)
    a1_mine, a1_mate = run_back(me, term1, head)
    sums, a1_mate, g0_got, g1_got = tie(sums, a1_mate, g0_got, g1_got)
    a1_got = send(a1_mate, CORE)
    sums = step(sums, X2)
    sums, a1_got = tie(sums, a1_got)
    p_keep, p_send, q_keep, q_send = run_fold(
        a0_mine, a0_got, g0_mine, g0_got, a1_mine, a1_got, g1_mine, g1_got
    )

    p_got, q_got = send(p_send, Y2), send(q_send, X2)
    sums = step(step(step(step(sums, CORE), ZL), ZH), Y1, Y2, Y3)
    sums, p_got, q_got = tie(sums, p_got, q_got)
    log_total, own, rest, pick = run_unpack(me, sums, weight)
    p_keep, p_send = run_combine(combine_p, rest, pick, p_keep, p_got)
    q_keep, q_send = run_combine(combine_q, rest, pick, q_keep, q_got)
    p_got, q_got = send(p_send, X2), send(q_send, Y2)
    log_total, p_keep = tie(log_total, p_keep)
    dlog = run_dlogits(me, capped0, capped1, log_total, weight, ids)
    head_grad = run_head_gradient(head_gradient_low, rows0, rows1, dlog)
    p_got, q_got, head_grad = tie(p_got, q_got, head_grad)
    keep, *outs = run_join(p_keep, p_got, q_keep, q_got)
    got = [send(out, partner) for out, partner in zip(outs, (X1, Y1, XY1))]
    head_grad = run_head_gradient(head_gradient_high, rows0, rows1, dlog, (head_grad,))
    *got, head_grad = tie(*got, head_grad)
    keep, *outs = run_split(me, keep, *got)
    z_got = tie(*(send(out, partner) for out, partner in zip(outs, (ZL, Z2, ZH))))
    hidden_grad = run_finish(keep, *z_got)
    return (own[:, 0], head_grad, hidden_grad)


def solution(mesh):
    in_specs = (P("dp", None), P(None, ("dp", "vocab")), P(), P())
    out_specs = (P("dp"), P(None, ("dp", "vocab")), P("dp", "vocab"))
    return jax.shard_map(local, mesh=mesh, in_specs=in_specs, out_specs=out_specs, check_vma=False)
```

```python
import jax
import jax.numpy as jnp
from jax import lax
from jax.experimental import pallas as pl
from jax.experimental.pallas import tpu as pltpu
from jax.sharding import PartitionSpec as P

softcap = 30.0
AXES = ("dp", "vocab")
bf16 = jnp.bfloat16
f32 = jnp.float32
D = 4608
WIDTH = 1024
FEATURES = 576
COLUMN = (512, 128)


def flips(core0, core1):
    return [(i, i ^ (core1 if i & 8 else core0)) for i in range(128)]


CORE = flips(8, 8)
XY1 = flips(16 ^ 1, 48 ^ 3)
X1, X2 = flips(16, 48), flips(48, 16)
Y1, Y2 = flips(1, 3), flips(3, 1)
X3, Y3 = flips(32, 32), flips(2, 2)
ZL, Z2, ZH = flips(4, 4), flips(64, 64), flips(68, 68)


def send(array, partner):
    return lax.ppermute(array, AXES, partner)


def slot_flip(slot, core):
    return (0, 1 + 2 * core, 3 - 2 * core, 2)[slot]


def whole_block(me, i):
    core = ((me >> 3) & 1) ^ ((i >> 2) & 1)
    x = ((me >> 4) & 3) ^ slot_flip(i & 3, core)
    return ((me >> 6) ^ (i >> 3)) * 8 + x * 2 + core


def feature_slot(me, i, other):
    core = ((me >> 3) & 1) ^ other
    apart = (me & 3) ^ (i & 3)
    return jnp.where(apart == 1 + 2 * core, 1, jnp.where(apart == 3 - 2 * core, 2, jnp.where(apart == 2, 3, 0)))


def call(kernel, ins, outs, scratch=(), flops=0, moved=0, mib=16, aliases={}):
    places = {"v": pltpu.VMEM, "s": pltpu.SMEM, "h": pl.ANY}
    return pl.pallas_call(
        kernel,
        in_specs=[pl.BlockSpec(memory_space=places[i]) for i in ins],
        out_specs=[pl.BlockSpec(memory_space=places[o[0]]) for o in outs],
        out_shape=[jax.ShapeDtypeStruct(o[1], o[2]) for o in outs],
        scratch_shapes=list(scratch),
        input_output_aliases=aliases,
        compiler_params=pltpu.CompilerParams(vmem_limit_bytes=mib << 20),
        cost_estimate=pl.CostEstimate(flops=flops, bytes_accessed=moved, transcendentals=0),
        name=kernel.__name__,
    )


def rows_of(i):
    return slice(32 * i, 32 * i + 32)


def from_lanes(row):
    return jnp.broadcast_to(row, (128, 128)).T


def local_block(me, i, whole):
    return whole[pl.ds(pl.multiple_of(whole_block(me, i) * 32, 32), 32), :]


def hits_of(me, ids, j):
    lane = lax.broadcasted_iota(jnp.int32, (ids.shape[0], 128), 1)
    return ids == (lane + (me * WIDTH + 128 * j)).astype(f32)


def forward(half, me_ref, *refs):
    pieces, (ids_ref, head_ref, rows, capped_ref, term_ref, total_ref, target_ref) = refs[:8], refs[8:]
    me = me_ref[0]
    for i in range(8):
        rows[rows_of(i), :] = pieces[i][...]
    ids = ids_ref[256 * half : 256 * half + 256, :]
    total = jnp.zeros((256, 128), f32)
    target = jnp.zeros((256, 128), f32)
    for n in range(4):
        raw = jnp.dot(rows[...], head_ref[:, 256 * n : 256 * n + 256], preferred_element_type=f32)
        ratio = jnp.tanh(raw / softcap)
        for j in range(2):
            start = 256 * n + 128 * j
            part = ratio[:, 128 * j : 128 * j + 128]
            capped = softcap * part
            expo = jnp.exp(capped)
            hit = hits_of(me, ids, 2 * n + j)
            capped_ref[:, start : start + 128] = capped
            term_ref[:, start : start + 128] = jnp.where(hit, 0.0, expo * (1.0 - part * part)).astype(bf16)
            total = total + expo
            target = target + jnp.where(hit, capped, 0.0)
    total_ref[...] = total
    target_ref[...] = target


def forward_low(*refs):
    forward(0, *refs)


def forward_high(*refs):
    forward(1, *refs)


def run_forward(kernel, me, pieces, ids, head):
    return call(
        kernel,
        "s" + "v" * 10,
        [
            ("v", (256, D), bf16),
            ("v", (256, WIDTH), f32),
            ("v", (256, WIDTH), bf16),
            ("v", (256, 128), f32),
            ("v", (256, 128), f32),
        ],
        flops=2 * 256 * D * WIDTH,
        moved=2 * D * WIDTH,
    )(me, *pieces, ids, head)


def pack(me_ref, total0, total1, target0, target1, out_ref, whole):
    me = me_ref[0]
    sums = []
    for halves in ((total0, total1), (target0, target1)):
        for i in range(16):
            spot = pl.ds(pl.multiple_of(whole_block(me, i) * 32, 32), 32)
            whole[spot, :] = halves[i // 8][rows_of(i % 8), :]
        for j in range(4):
            sums.append(jnp.sum(whole[128 * j : 128 * j + 128, :].T, axis=0, keepdims=True))
    out_ref[...] = jnp.concatenate(sums, axis=0)


def run_pack(me, *columns):
    return call(pack, "svvvv", [("v", (8, 128), f32)], scratch=[pltpu.VMEM(COLUMN, f32)], moved=1 << 20)(
        me, *columns
    )[0]


def unpack(me_ref, sums_ref, weight_ref, log_ref, own_ref, rest_ref, pick_ref, logs, targets):
    me = me_ref[0]
    sums = sums_ref[...]
    for j in range(4):
        logs[128 * j : 128 * j + 128, :] = from_lanes(jnp.log(sums[j : j + 1, :]))
        targets[128 * j : 128 * j + 128, :] = from_lanes(sums[4 + j : 5 + j, :])
    for i in range(16):
        log_ref[rows_of(i), :] = local_block(me, i, logs)
    own_ref[...] = local_block(me, 0, targets) - local_block(me, 0, logs)
    for zr in range(2):
        for x in range(4):
            i = 8 * zr + x
            log_total = log_ref[rows_of(i), :]
            target = local_block(me, i, targets)
            weight = weight_ref[rows_of(i), :]
            ratio = target / softcap
            rest_ref[rows_of(4 * zr + x), :] = weight * jnp.exp(-log_total)
            pick_ref[rows_of(4 * zr + x), :] = weight * (jnp.exp(target - log_total) - 1.0) * (1.0 - ratio * ratio)


def run_unpack(me, sums, weight):
    outs = [("v", COLUMN, f32), ("v", (32, 128), f32), ("v", (256, 128), f32), ("v", (256, 128), f32)]
    return call(unpack, "svv", outs, scratch=[pltpu.VMEM(COLUMN, f32)] * 2, moved=1 << 20)(me, sums, weight)


def back_part(me, n, rows, head_ref, mine_ref, mate_ref):
    out = lax.dot_general(
        rows, head_ref[1152 * n : 1152 * n + 1152, :], (((1,), (1,)), ((), ())), preferred_element_type=f32
    ).astype(bf16)
    for i in range(2):
        part = out[:, FEATURES * i : FEATURES * i + FEATURES]
        block = 2 * n + i
        spot = slice(FEATURES * (block // 4), FEATURES * (block // 4) + FEATURES)
        mine_ref[feature_slot(me, block, 0), :, :, spot] = part[:128].reshape(4, 32, FEATURES)
        mate_ref[feature_slot(me, block, 1), :, :, spot] = part[128:].reshape(4, 32, FEATURES)


def back(me_ref, rows_ref, head_ref, mine_ref, mate_ref):
    for n in range(4):
        back_part(me_ref[0], n, rows_ref[...], head_ref, mine_ref, mate_ref)


BLOCKS = ("v", (4, 4, 32, 2 * FEATURES), bf16)
BACK_COST = dict(flops=2 * 256 * D * WIDTH, moved=2 * D * WIDTH)


def run_back(me, rows, head):
    return call(back, "svv", [BLOCKS, BLOCKS], **BACK_COST)(me, rows, head)


def begin(me_ref, ids_ref, weight_ref, head_ref, mine0, mate0, mine1, mate1, held_ref, ids_out, weight_out, *scratch):
    ids_near, weight_near, ids_whole, weight_whole, rows, sems = scratch
    me = me_ref[0]
    small = [
        pltpu.make_async_copy(ids_ref, ids_near, sems.at[4]),
        pltpu.make_async_copy(weight_ref, weight_near, sems.at[5]),
    ]
    loads = []
    for n in range(4):
        spot = pl.ds(1152 * n, 1152)
        loads.append(pltpu.make_async_copy(head_ref.at[spot], held_ref.at[spot], sems.at[n]))
    for copy in small + loads:
        copy.start()
    for copy in small:
        copy.wait()
    for j in range(4):
        ids_whole[128 * j : 128 * j + 128, :] = from_lanes(ids_near[j : j + 1, :].astype(f32))
        weight_whole[128 * j : 128 * j + 128, :] = from_lanes(weight_near[j : j + 1, :])
    for i in range(16):
        ids_out[rows_of(i), :] = local_block(me, i, ids_whole)
        weight_out[rows_of(i), :] = local_block(me, i, weight_whole)
    ids = ids_out[...]
    for j in range(WIDTH // 128):
        rows[:, 128 * j : 128 * j + 128] = jnp.where(hits_of(me, ids, j), 1.0, 0.0).astype(bf16)
    for n in range(4):
        loads[n].wait()
        for half, (mine, mate) in enumerate(((mine0, mate0), (mine1, mate1))):
            back_part(me, n, rows[256 * half : 256 * half + 256, :], held_ref, mine, mate)


def run_begin(me, ids, weight, head):
    column = ("v", COLUMN, f32)
    return call(
        begin,
        "shhh",
        [BLOCKS] * 4 + [("v", (D, WIDTH), bf16), column, column],
        scratch=[
            pltpu.VMEM((4, 128), jnp.int32),
            pltpu.VMEM((4, 128), f32),
            pltpu.VMEM(COLUMN, f32),
            pltpu.VMEM(COLUMN, f32),
            pltpu.VMEM((512, WIDTH), bf16),
            pltpu.SemaphoreType.DMA((6,)),
        ],
        flops=4 * 256 * D * WIDTH,
        moved=2 * D * WIDTH,
    )(me, *(pltpu.with_memory_space_constraint(array, pltpu.HBM) for array in (ids, weight, head)))


def fold(*refs):
    parts, (p_keep, p_send, q_keep, q_send) = refs[:8], refs[8:]
    for zr in range(2):
        a_mine, a_got, g_mine, g_got = parts[4 * zr : 4 * zr + 4]
        for k in range(4):
            for x in range(4):
                p_at = (p_keep if k < 2 else p_send).at[x // 2, k % 2, x % 2, zr]
                q_at = (q_keep if x < 2 else q_send).at[k // 2, k % 2, x % 2, zr]
                for first, mine, got in ((0, a_mine, a_got), (16, g_mine, g_got)):
                    total = mine[k, x] + got[k, x]
                    p_at[first : first + 16] = total[:16]
                    q_at[first : first + 16] = total[16:]


def run_fold(*parts):
    return call(fold, "v" * 8, [("v", (2, 2, 2, 2, 32, 2 * FEATURES), bf16)] * 4, moved=512 * D * 8)(*parts)


def combine(first_row, slots, rest_ref, pick_ref, held, got, keep, out):
    for h, target in enumerate((keep, out)):
        for i in range(2):
            for j in range(2):
                x = slots(h, j)
                for zr in range(2):
                    first = 128 * zr + 32 * x + first_row
                    rest = rest_ref[first : first + 16, :]
                    pick = pick_ref[first : first + 16, :]
                    for start in range(0, 2 * FEATURES, 128):
                        at = (h, i, j, zr, slice(None), slice(start, start + 128))
                        both = (held[at] + got[at]).astype(f32)
                        target[at[1:]] = (rest * both[:16] + pick * both[16:]).astype(bf16)


def combine_p(*refs):
    combine(0, lambda h, j: 2 * h + j, *refs)


def combine_q(*refs):
    combine(16, lambda h, j: j, *refs)


def run_combine(kernel, *parts):
    half = ("v", (2, 2, 2, 16, 2 * FEATURES), bf16)
    return call(kernel, "v" * 4, [half, half], moved=1 << 22)(*parts)


def join(p_keep, p_got, q_keep, q_got, *outs):
    for n, out in enumerate(outs):
        out[:, :16] = p_keep[n // 2, n % 2] + p_got[n // 2, n % 2]
        out[:, 16:] = q_keep[n // 2, n % 2] + q_got[n // 2, n % 2]


def run_join(*parts):
    return call(join, "v" * 4, [("v", (2, 32, 2 * FEATURES), bf16)] * 4, moved=1 << 22)(*parts)


def split(me_ref, *refs):
    terms, outs = refs[:4], refs[4:]
    low = ((me_ref[0] >> 2) & 1) == 0
    for zr in range(2):
        total = sum(term[zr].astype(f32) for term in terms)
        halves = (total[:, :FEATURES], total[:, FEATURES:])
        for zl in range(2):
            outs[2 * zr + zl][...] = jnp.where(low, halves[zl], halves[1 - zl]).astype(bf16)


def run_split(me, *parts):
    return call(split, "svvvv", [("v", (32, FEATURES), bf16)] * 4, moved=1 << 20)(me, *parts)


def finish(*refs):
    terms, out_ref = refs[:4], refs[4]
    out_ref[...] = sum(term[...].astype(f32) for term in terms).astype(bf16)


def run_finish(*terms):
    return call(finish, "v" * 4, [("v", (32, FEATURES), bf16)], moved=1 << 17)(*terms)[0]


def dlogits(me_ref, low_ref, high_ref, log_ref, weight_ref, ids_ref, out_ref):
    me = me_ref[0]
    for n in range(4):
        capped_ref = low_ref if n < 2 else high_ref
        rows = slice(128 * (n % 2), 128 * (n % 2) + 128)
        out_rows = slice(128 * n, 128 * n + 128)
        log_total = log_ref[out_rows, :]
        weight = weight_ref[out_rows, :]
        ids = ids_ref[out_rows, :]
        for j in range(WIDTH // 128):
            spot = slice(128 * j, 128 * j + 128)
            capped = capped_ref[rows, spot]
            prob = jnp.exp(capped - log_total)
            onehot = jnp.where(hits_of(me, ids, j), 1.0, 0.0)
            ratio = capped / softcap
            out_ref[out_rows, spot] = (weight * (prob - onehot) * (1.0 - ratio * ratio)).astype(bf16)


def run_dlogits(me, low, high, log_total, weight, ids):
    return call(
        dlogits, "svvvvv", [("v", (512, WIDTH), bf16)], flops=512 * WIDTH * 16, moved=6 * 512 * WIDTH
    )(me, low, high, log_total, weight, ids)[0]


def head_rows(first, last, low_ref, high_ref, dlog_ref, out_ref, rows, buffer, sems):
    def copy(i):
        return pltpu.make_async_copy(buffer.at[i % 2], out_ref.at[pl.ds(512 * i, 512)], sems.at[i % 2])

    for i in range(first, last):
        spot = slice(512 * i, 512 * i + 512)
        rows[:256, :] = low_ref[:, spot]
        rows[256:, :] = high_ref[:, spot]
        if i >= first + 2:
            copy(i - 2).wait()
        buffer[i % 2] = lax.dot_general(
            rows[...], dlog_ref[...], (((0,), (0,)), ((), ())), preferred_element_type=f32
        ).astype(bf16)
        copy(i).start()
    copy(last - 2).wait()
    copy(last - 1).wait()


def head_gradient_low(low_ref, high_ref, dlog_ref, out_ref, *scratch):
    head_rows(0, 5, low_ref, high_ref, dlog_ref, out_ref, *scratch)


def head_gradient_high(low_ref, high_ref, dlog_ref, started_ref, out_ref, *scratch):
    head_rows(5, 9, low_ref, high_ref, dlog_ref, out_ref, *scratch)


def run_head_gradient(kernel, low, high, dlog, started=()):
    return call(
        kernel,
        "vvv" + "h" * len(started),
        [("h", (D, WIDTH), bf16)],
        scratch=[
            pltpu.VMEM((512, 512), bf16),
            pltpu.VMEM((2, 512, WIDTH), bf16),
            pltpu.SemaphoreType.DMA((2,)),
        ],
        flops=512 * WIDTH * D,
        moved=D * WIDTH,
        aliases={3: 0} if started else {},
    )(low, high, dlog, *started)[0]


def tie(*arrays):
    return lax.optimization_barrier(arrays)


def local(hidden, head, verdict_ids, row_weight):
    me = (lax.axis_index("dp") * 8 + lax.axis_index("vocab")).astype(jnp.int32).reshape(1)
    a1, a2, a3 = send(hidden, X1), send(hidden, X2), send(hidden, X3)
    o0 = send(hidden, ZH)
    g0_mine, g0_mate, g1_mine, g1_mate, head, ids, weight = run_begin(
        me, verdict_ids.reshape(4, 128), row_weight.reshape(4, 128), head
    )
    o0, a3, a2, a1, g0_mine, g0_mate, g1_mine, g1_mate = tie(o0, a3, a2, a1, g0_mine, g0_mate, g1_mine, g1_mate)
    o1, o2, o3 = send(o0, X1), send(o0, X2), send(a3, ZH)
    own_half = [hidden, a1, a2, a3]
    own_half += [send(piece, CORE) for piece in own_half]
    rows0, capped0, term0, total0, target0 = run_forward(forward_low, me, own_half, ids, head)
    o1, term0 = tie(o1, term0)
    a0_mine, a0_mate = run_back(me, term0, head)
    o1, o3, o2, a0_mate = tie(o1, o3, o2, a0_mate)
    other_half = [o0, o1, o2, o3]
    *swapped, a0_mate = tie(*(send(piece, CORE) for piece in other_half), a0_mate)
    other_half += swapped
    a0_got = send(a0_mate, CORE)
    rows1, capped1, term1, total1, target1 = run_forward(forward_high, me, other_half, ids, head)

    def step(sums, *partners):
        got = tie(*(send(sums, partner) for partner in partners))
        return sums + sum(got)

    total1, a0_got, g0_mate, g1_mate = tie(total1, a0_got, g0_mate, g1_mate)
    g0_got, g1_got = send(g0_mate, CORE), send(g1_mate, CORE)
    sums = step(run_pack(me, total0, total1, target0, target1), X1)
    a1_mine, a1_mate = run_back(me, term1, head)
    sums, a1_mate, g0_got, g1_got = tie(sums, a1_mate, g0_got, g1_got)
    a1_got = send(a1_mate, CORE)
    sums = step(sums, X2)
    a1_got, sums = tie(a1_got, sums)
    p_keep, p_send, q_keep, q_send = run_fold(
        a0_mine, a0_got, g0_mine, g0_got, a1_mine, a1_got, g1_mine, g1_got
    )
    sums = step(sums, CORE)
    p_send, q_send, sums = tie(p_send, q_send, sums)

    p_got, q_got = send(p_send, Y2), send(q_send, X2)
    sums = step(step(step(sums, ZL), ZH), Y1, Y2, Y3)
    sums, p_got, q_got = tie(sums, p_got, q_got)
    log_total, own, rest, pick = run_unpack(me, sums, weight)
    p_keep, p_send = run_combine(combine_p, rest, pick, p_keep, p_got)
    q_keep, q_send = run_combine(combine_q, rest, pick, q_keep, q_got)
    p_got, q_got = send(p_send, X2), send(q_send, Y2)
    log_total, p_keep = tie(log_total, p_keep)
    dlog = run_dlogits(me, capped0, capped1, log_total, weight, ids)
    head_grad = run_head_gradient(head_gradient_low, rows0, rows1, dlog)
    p_got, q_got, head_grad = tie(p_got, q_got, head_grad)
    keep, *outs = run_join(p_keep, p_got, q_keep, q_got)
    got = [send(out, partner) for out, partner in zip(outs, (X1, Y1, XY1))]
    head_grad = run_head_gradient(head_gradient_high, rows0, rows1, dlog, (head_grad,))
    *got, head_grad = tie(*got, head_grad)
    keep, *outs = run_split(me, keep, *got)
    z_got = tie(send(outs[1], Z2), send(outs[0], ZL), send(outs[2], ZH))
    hidden_grad = run_finish(keep, *z_got)
    return (own[:, 0], head_grad, hidden_grad)


def solution(mesh):
    in_specs = (P("dp", None), P(None, ("dp", "vocab")), P(), P())
    out_specs = (P("dp"), P(None, ("dp", "vocab")), P("dp", "vocab"))
    return jax.shard_map(local, mesh=mesh, in_specs=in_specs, out_specs=out_specs, check_vma=False)
```

```python
import jax
import jax.numpy as jnp
from jax import lax
from jax.experimental import pallas as pl
from jax.experimental.pallas import tpu as pltpu
from jax.sharding import PartitionSpec as P

softcap = 30.0
AXES = ("dp", "vocab")
bf16 = jnp.bfloat16
f32 = jnp.float32
D = 4608
WIDTH = 1024
FEATURES = 576
COLUMN = (512, 128)


def flips(core0, core1):
    return [(i, i ^ (core1 if i & 8 else core0)) for i in range(128)]


CORE = flips(8, 8)
XY1 = flips(16 ^ 1, 48 ^ 3)
X1, X2 = flips(16, 48), flips(48, 16)
Y1, Y2 = flips(1, 3), flips(3, 1)
X3, Y3 = flips(32, 32), flips(2, 2)
ZL, Z2, ZH = flips(4, 4), flips(64, 64), flips(68, 68)


def send(array, partner):
    return lax.ppermute(array, AXES, partner)


def slot_flip(slot, core):
    return (0, 1 + 2 * core, 3 - 2 * core, 2)[slot]


def whole_block(me, i):
    core = ((me >> 3) & 1) ^ ((i >> 2) & 1)
    x = ((me >> 4) & 3) ^ slot_flip(i & 3, core)
    return ((me >> 6) ^ (i >> 3)) * 8 + x * 2 + core


def feature_slot(me, i, other):
    core = ((me >> 3) & 1) ^ other
    apart = (me & 3) ^ (i & 3)
    return jnp.where(apart == 1 + 2 * core, 1, jnp.where(apart == 3 - 2 * core, 2, jnp.where(apart == 2, 3, 0)))


def call(kernel, ins, outs, scratch=(), flops=0, moved=0, mib=16, aliases={}):
    places = {"v": pltpu.VMEM, "s": pltpu.SMEM, "h": pl.ANY}
    return pl.pallas_call(
        kernel,
        in_specs=[pl.BlockSpec(memory_space=places[i]) for i in ins],
        out_specs=[pl.BlockSpec(memory_space=places[o[0]]) for o in outs],
        out_shape=[jax.ShapeDtypeStruct(o[1], o[2]) for o in outs],
        scratch_shapes=list(scratch),
        input_output_aliases=aliases,
        compiler_params=pltpu.CompilerParams(vmem_limit_bytes=mib << 20),
        cost_estimate=pl.CostEstimate(flops=flops, bytes_accessed=moved, transcendentals=0),
        name=kernel.__name__,
    )


def rows_of(i):
    return slice(32 * i, 32 * i + 32)


def from_lanes(row):
    return jnp.broadcast_to(row, (128, 128)).T


def local_block(me, i, whole):
    return whole[pl.ds(pl.multiple_of(whole_block(me, i) * 32, 32), 32), :]


def hits_of(me, ids, j):
    lane = lax.broadcasted_iota(jnp.int32, (ids.shape[0], 128), 1)
    return ids == (lane + (me * WIDTH + 128 * j)).astype(f32)


def forward(half, me_ref, *refs):
    pieces, (ids_ref, head_ref, rows, capped_ref, term_ref, total_ref, target_ref) = refs[:8], refs[8:]
    me = me_ref[0]
    for i in range(8):
        rows[rows_of(i), :] = pieces[i][...]
    ids = ids_ref[256 * half : 256 * half + 256, :]
    total = jnp.zeros((256, 128), f32)
    target = jnp.zeros((256, 128), f32)
    for n in range(4):
        raw = jnp.dot(rows[...], head_ref[:, 256 * n : 256 * n + 256], preferred_element_type=f32)
        ratio = jnp.tanh(raw / softcap)
        for j in range(2):
            start = 256 * n + 128 * j
            part = ratio[:, 128 * j : 128 * j + 128]
            capped = softcap * part
            expo = jnp.exp(capped)
            hit = hits_of(me, ids, 2 * n + j)
            capped_ref[:, start : start + 128] = capped
            term_ref[:, start : start + 128] = jnp.where(hit, 0.0, expo * (1.0 - part * part)).astype(bf16)
            total = total + expo
            target = target + jnp.where(hit, capped, 0.0)
    total_ref[...] = total
    target_ref[...] = target


def forward_low(*refs):
    forward(0, *refs)


def forward_high(*refs):
    forward(1, *refs)


def run_forward(kernel, me, pieces, ids, head):
    return call(
        kernel,
        "s" + "v" * 10,
        [
            ("v", (256, D), bf16),
            ("v", (256, WIDTH), f32),
            ("v", (256, WIDTH), bf16),
            ("v", (256, 128), f32),
            ("v", (256, 128), f32),
        ],
        flops=2 * 256 * D * WIDTH,
        moved=2 * D * WIDTH,
    )(me, *pieces, ids, head)


def pack(me_ref, total0, total1, target0, target1, out_ref, whole):
    me = me_ref[0]
    sums = []
    for halves in ((total0, total1), (target0, target1)):
        for i in range(16):
            spot = pl.ds(pl.multiple_of(whole_block(me, i) * 32, 32), 32)
            whole[spot, :] = halves[i // 8][rows_of(i % 8), :]
        for j in range(4):
            sums.append(jnp.sum(whole[128 * j : 128 * j + 128, :].T, axis=0, keepdims=True))
    out_ref[...] = jnp.concatenate(sums, axis=0)


def run_pack(me, *columns):
    return call(pack, "svvvv", [("v", (8, 128), f32)], scratch=[pltpu.VMEM(COLUMN, f32)], moved=1 << 20)(
        me, *columns
    )[0]


def unpack(me_ref, sums_ref, weight_ref, log_ref, own_ref, rest_ref, pick_ref, logs, targets):
    me = me_ref[0]
    sums = sums_ref[...]
    for j in range(4):
        logs[128 * j : 128 * j + 128, :] = from_lanes(jnp.log(sums[j : j + 1, :]))
        targets[128 * j : 128 * j + 128, :] = from_lanes(sums[4 + j : 5 + j, :])
    for i in range(16):
        log_ref[rows_of(i), :] = local_block(me, i, logs)
    own_ref[...] = local_block(me, 0, targets) - local_block(me, 0, logs)
    for zr in range(2):
        for x in range(4):
            i = 8 * zr + x
            log_total = log_ref[rows_of(i), :]
            target = local_block(me, i, targets)
            weight = weight_ref[rows_of(i), :]
            ratio = target / softcap
            rest_ref[rows_of(4 * zr + x), :] = weight * jnp.exp(-log_total)
            pick_ref[rows_of(4 * zr + x), :] = weight * (jnp.exp(target - log_total) - 1.0) * (1.0 - ratio * ratio)


def run_unpack(me, sums, weight):
    outs = [("v", COLUMN, f32), ("v", (32, 128), f32), ("v", (256, 128), f32), ("v", (256, 128), f32)]
    return call(unpack, "svv", outs, scratch=[pltpu.VMEM(COLUMN, f32)] * 2, moved=1 << 20)(me, sums, weight)


def back_part(me, n, rows, head_ref, mine_ref, mate_ref):
    out = lax.dot_general(
        rows, head_ref[1152 * n : 1152 * n + 1152, :], (((1,), (1,)), ((), ())), preferred_element_type=f32
    ).astype(bf16)
    for i in range(2):
        part = out[:, FEATURES * i : FEATURES * i + FEATURES]
        block = 2 * n + i
        spot = slice(FEATURES * (block // 4), FEATURES * (block // 4) + FEATURES)
        mine_ref[feature_slot(me, block, 0), :, :, spot] = part[:128].reshape(4, 32, FEATURES)
        mate_ref[feature_slot(me, block, 1), :, :, spot] = part[128:].reshape(4, 32, FEATURES)


def back(me_ref, rows_ref, head_ref, mine_ref, mate_ref):
    for n in range(4):
        back_part(me_ref[0], n, rows_ref[...], head_ref, mine_ref, mate_ref)


BLOCKS = ("v", (4, 4, 32, 2 * FEATURES), bf16)
BACK_COST = dict(flops=2 * 256 * D * WIDTH, moved=2 * D * WIDTH)


def run_back(me, rows, head):
    return call(back, "svv", [BLOCKS, BLOCKS], **BACK_COST)(me, rows, head)


def begin(me_ref, ids_ref, weight_ref, head_ref, mine0, mate0, mine1, mate1, held_ref, ids_out, weight_out, *scratch):
    ids_near, weight_near, ids_whole, weight_whole, rows, sems = scratch
    me = me_ref[0]
    small = [
        pltpu.make_async_copy(ids_ref, ids_near, sems.at[4]),
        pltpu.make_async_copy(weight_ref, weight_near, sems.at[5]),
    ]
    loads = []
    for n in range(4):
        spot = pl.ds(1152 * n, 1152)
        loads.append(pltpu.make_async_copy(head_ref.at[spot], held_ref.at[spot], sems.at[n]))
    for copy in small + loads:
        copy.start()
    for copy in small:
        copy.wait()
    for j in range(4):
        ids_whole[128 * j : 128 * j + 128, :] = from_lanes(ids_near[j : j + 1, :].astype(f32))
        weight_whole[128 * j : 128 * j + 128, :] = from_lanes(weight_near[j : j + 1, :])
    for i in range(16):
        ids_out[rows_of(i), :] = local_block(me, i, ids_whole)
        weight_out[rows_of(i), :] = local_block(me, i, weight_whole)
    ids = ids_out[...]
    for j in range(WIDTH // 128):
        rows[:, 128 * j : 128 * j + 128] = jnp.where(hits_of(me, ids, j), 1.0, 0.0).astype(bf16)
    for n in range(4):
        loads[n].wait()
        for half, (mine, mate) in enumerate(((mine0, mate0), (mine1, mate1))):
            back_part(me, n, rows[256 * half : 256 * half + 256, :], held_ref, mine, mate)


def run_begin(me, ids, weight, head):
    column = ("v", COLUMN, f32)
    return call(
        begin,
        "shhh",
        [BLOCKS] * 4 + [("v", (D, WIDTH), bf16), column, column],
        scratch=[
            pltpu.VMEM((4, 128), jnp.int32),
            pltpu.VMEM((4, 128), f32),
            pltpu.VMEM(COLUMN, f32),
            pltpu.VMEM(COLUMN, f32),
            pltpu.VMEM((512, WIDTH), bf16),
            pltpu.SemaphoreType.DMA((6,)),
        ],
        flops=4 * 256 * D * WIDTH,
        moved=2 * D * WIDTH,
    )(me, *(pltpu.with_memory_space_constraint(array, pltpu.HBM) for array in (ids, weight, head)))


def fold(*refs):
    parts, (p_keep, p_send, q_keep, q_send) = refs[:8], refs[8:]
    for zr in range(2):
        a_mine, a_got, g_mine, g_got = parts[4 * zr : 4 * zr + 4]
        for k in range(4):
            for x in range(4):
                p_at = (p_keep if k < 2 else p_send).at[x // 2, k % 2, x % 2, zr]
                q_at = (q_keep if x < 2 else q_send).at[k // 2, k % 2, x % 2, zr]
                for first, mine, got in ((0, a_mine, a_got), (16, g_mine, g_got)):
                    total = mine[k, x] + got[k, x]
                    p_at[first : first + 16] = total[:16]
                    q_at[first : first + 16] = total[16:]


def run_fold(*parts):
    return call(fold, "v" * 8, [("v", (2, 2, 2, 2, 32, 2 * FEATURES), bf16)] * 4, moved=512 * D * 8)(*parts)


def combine(first_row, slots, rest_ref, pick_ref, held, got, keep, out):
    for h, target in enumerate((keep, out)):
        for i in range(2):
            for j in range(2):
                x = slots(h, j)
                for zr in range(2):
                    first = 128 * zr + 32 * x + first_row
                    rest = rest_ref[first : first + 16, :]
                    pick = pick_ref[first : first + 16, :]
                    for start in range(0, 2 * FEATURES, 128):
                        at = (h, i, j, zr, slice(None), slice(start, start + 128))
                        both = (held[at] + got[at]).astype(f32)
                        target[at[1:]] = (rest * both[:16] + pick * both[16:]).astype(bf16)


def combine_p(*refs):
    combine(0, lambda h, j: 2 * h + j, *refs)


def combine_q(*refs):
    combine(16, lambda h, j: j, *refs)


def run_combine(kernel, *parts):
    half = ("v", (2, 2, 2, 16, 2 * FEATURES), bf16)
    return call(kernel, "v" * 4, [half, half], moved=1 << 22)(*parts)


def join(p_keep, p_got, q_keep, q_got, *outs):
    for n, out in enumerate(outs):
        out[:, :16] = p_keep[n // 2, n % 2] + p_got[n // 2, n % 2]
        out[:, 16:] = q_keep[n // 2, n % 2] + q_got[n // 2, n % 2]


def run_join(*parts):
    return call(join, "v" * 4, [("v", (2, 32, 2 * FEATURES), bf16)] * 4, moved=1 << 22)(*parts)


def split(me_ref, *refs):
    terms, outs = refs[:4], refs[4:]
    low = ((me_ref[0] >> 2) & 1) == 0
    for zr in range(2):
        total = sum(term[zr].astype(f32) for term in terms)
        halves = (total[:, :FEATURES], total[:, FEATURES:])
        for zl in range(2):
            outs[2 * zr + zl][...] = jnp.where(low, halves[zl], halves[1 - zl]).astype(bf16)


def run_split(me, *parts):
    return call(split, "svvvv", [("v", (32, FEATURES), bf16)] * 4, moved=1 << 20)(me, *parts)


def finish(*refs):
    terms, out_ref = refs[:4], refs[4]
    out_ref[...] = sum(term[...].astype(f32) for term in terms).astype(bf16)


def run_finish(*terms):
    return call(finish, "v" * 4, [("v", (32, FEATURES), bf16)], moved=1 << 17)(*terms)[0]


def dlogits(me_ref, low_ref, high_ref, log_ref, weight_ref, ids_ref, out_ref):
    me = me_ref[0]
    for n in range(4):
        capped_ref = low_ref if n < 2 else high_ref
        rows = slice(128 * (n % 2), 128 * (n % 2) + 128)
        out_rows = slice(128 * n, 128 * n + 128)
        log_total = log_ref[out_rows, :]
        weight = weight_ref[out_rows, :]
        ids = ids_ref[out_rows, :]
        for j in range(WIDTH // 128):
            spot = slice(128 * j, 128 * j + 128)
            capped = capped_ref[rows, spot]
            prob = jnp.exp(capped - log_total)
            onehot = jnp.where(hits_of(me, ids, j), 1.0, 0.0)
            ratio = capped / softcap
            out_ref[out_rows, spot] = (weight * (prob - onehot) * (1.0 - ratio * ratio)).astype(bf16)


def run_dlogits(me, low, high, log_total, weight, ids):
    return call(
        dlogits, "svvvvv", [("v", (512, WIDTH), bf16)], flops=512 * WIDTH * 16, moved=6 * 512 * WIDTH
    )(me, low, high, log_total, weight, ids)[0]


def head_rows(first, last, low_ref, high_ref, dlog_ref, out_ref, rows, buffer, sems):
    def copy(i):
        return pltpu.make_async_copy(buffer.at[i % 2], out_ref.at[pl.ds(512 * i, 512)], sems.at[i % 2])

    for i in range(first, last):
        spot = slice(512 * i, 512 * i + 512)
        rows[:256, :] = low_ref[:, spot]
        rows[256:, :] = high_ref[:, spot]
        if i >= first + 2:
            copy(i - 2).wait()
        buffer[i % 2] = lax.dot_general(
            rows[...], dlog_ref[...], (((0,), (0,)), ((), ())), preferred_element_type=f32
        ).astype(bf16)
        copy(i).start()
    copy(last - 2).wait()
    copy(last - 1).wait()


def head_gradient_low(low_ref, high_ref, dlog_ref, out_ref, *scratch):
    head_rows(0, 5, low_ref, high_ref, dlog_ref, out_ref, *scratch)


def head_gradient_mid(low_ref, high_ref, dlog_ref, started_ref, out_ref, *scratch):
    head_rows(5, 7, low_ref, high_ref, dlog_ref, out_ref, *scratch)


def head_gradient_high(low_ref, high_ref, dlog_ref, started_ref, out_ref, *scratch):
    head_rows(7, 9, low_ref, high_ref, dlog_ref, out_ref, *scratch)


def run_head_gradient(kernel, low, high, dlog, started=()):
    return call(
        kernel,
        "vvv" + "h" * len(started),
        [("h", (D, WIDTH), bf16)],
        scratch=[
            pltpu.VMEM((512, 512), bf16),
            pltpu.VMEM((2, 512, WIDTH), bf16),
            pltpu.SemaphoreType.DMA((2,)),
        ],
        flops=512 * WIDTH * D,
        moved=D * WIDTH,
        aliases={3: 0} if started else {},
    )(low, high, dlog, *started)[0]


def tie(*arrays):
    return lax.optimization_barrier(arrays)


def local(hidden, head, verdict_ids, row_weight):
    me = (lax.axis_index("dp") * 8 + lax.axis_index("vocab")).astype(jnp.int32).reshape(1)
    a1, a2, a3 = send(hidden, X1), send(hidden, X2), send(hidden, X3)
    o0 = send(hidden, ZH)
    g0_mine, g0_mate, g1_mine, g1_mate, head, ids, weight = run_begin(
        me, verdict_ids.reshape(4, 128), row_weight.reshape(4, 128), head
    )
    o0, a3, a2, a1, g0_mine, g0_mate, g1_mine, g1_mate = tie(o0, a3, a2, a1, g0_mine, g0_mate, g1_mine, g1_mate)
    o1, o2, o3 = send(o0, X1), send(o0, X2), send(a3, ZH)
    own_half = [hidden, a1, a2, a3]
    own_half += [send(piece, CORE) for piece in own_half]
    rows0, capped0, term0, total0, target0 = run_forward(forward_low, me, own_half, ids, head)
    o1, term0 = tie(o1, term0)
    a0_mine, a0_mate = run_back(me, term0, head)
    o1, o3, o2, a0_mate = tie(o1, o3, o2, a0_mate)
    other_half = [o0, o1, o2, o3]
    *swapped, a0_mate = tie(*(send(piece, CORE) for piece in other_half), a0_mate)
    other_half += swapped
    a0_got = send(a0_mate, CORE)
    rows1, capped1, term1, total1, target1 = run_forward(forward_high, me, other_half, ids, head)

    def step(sums, *partners):
        got = tie(*(send(sums, partner) for partner in partners))
        return sums + sum(got)

    total1, a0_got, g0_mate, g1_mate = tie(total1, a0_got, g0_mate, g1_mate)
    g0_got, g1_got = send(g0_mate, CORE), send(g1_mate, CORE)
    sums = step(run_pack(me, total0, total1, target0, target1), X1)
    a1_mine, a1_mate = run_back(me, term1, head)
    sums, a1_mate, g0_got, g1_got = tie(sums, a1_mate, g0_got, g1_got)
    a1_got = send(a1_mate, CORE)
    sums = step(sums, X2)
    a1_got, sums = tie(a1_got, sums)
    p_keep, p_send, q_keep, q_send = run_fold(
        a0_mine, a0_got, g0_mine, g0_got, a1_mine, a1_got, g1_mine, g1_got
    )
    sums = step(sums, CORE)
    p_send, q_send, sums = tie(p_send, q_send, sums)

    p_got, q_got = send(p_send, Y2), send(q_send, X2)
    sums = step(step(step(sums, ZL), ZH), Y1, Y2, Y3)
    sums, p_got, q_got = tie(sums, p_got, q_got)
    log_total, own, rest, pick = run_unpack(me, sums, weight)
    p_keep, p_send = run_combine(combine_p, rest, pick, p_keep, p_got)
    q_keep, q_send = run_combine(combine_q, rest, pick, q_keep, q_got)
    p_got, q_got = send(p_send, X2), send(q_send, Y2)
    log_total, p_keep = tie(log_total, p_keep)
    dlog = run_dlogits(me, capped0, capped1, log_total, weight, ids)
    head_grad = run_head_gradient(head_gradient_low, rows0, rows1, dlog)
    p_got, q_got, head_grad = tie(p_got, q_got, head_grad)
    keep, *outs = run_join(p_keep, p_got, q_keep, q_got)
    got = [send(out, partner) for out, partner in zip(outs, (X1, Y1, XY1))]
    head_grad = run_head_gradient(head_gradient_mid, rows0, rows1, dlog, (head_grad,))
    *got, head_grad = tie(*got, head_grad)
    keep, *outs = run_split(me, keep, *got)
    z_got = send(outs[1], Z2), send(outs[0], ZL), send(outs[2], ZH)
    head_grad = run_head_gradient(head_gradient_high, rows0, rows1, dlog, (head_grad,))
    *z_got, head_grad = tie(*z_got, head_grad)
    hidden_grad = run_finish(keep, *z_got)
    return (own[:, 0], head_grad, hidden_grad)


def solution(mesh):
    in_specs = (P("dp", None), P(None, ("dp", "vocab")), P(), P())
    out_specs = (P("dp"), P(None, ("dp", "vocab")), P("dp", "vocab"))
    return jax.shard_map(local, mesh=mesh, in_specs=in_specs, out_specs=out_specs, check_vma=False)
```

```python
import jax
import jax.numpy as jnp
from jax import lax
from jax.experimental import pallas as pl
from jax.experimental.pallas import tpu as pltpu
from jax.sharding import PartitionSpec as P

softcap = 30.0
AXES = ("dp", "vocab")
bf16 = jnp.bfloat16
f32 = jnp.float32
D = 4608
WIDTH = 1024
FEATURES = 576
COLUMN = (512, 128)


def flips(core0, core1):
    return [(i, i ^ (core1 if i & 8 else core0)) for i in range(128)]


CORE = flips(8, 8)
XY1 = flips(16 ^ 1, 48 ^ 3)
X1, X2 = flips(16, 48), flips(48, 16)
Y1, Y2 = flips(1, 3), flips(3, 1)
X3, Y3 = flips(32, 32), flips(2, 2)
ZL, Z2, ZH = flips(4, 4), flips(64, 64), flips(68, 68)


def send(array, partner):
    return lax.ppermute(array, AXES, partner)


def slot_flip(slot, core):
    return (0, 1 + 2 * core, 3 - 2 * core, 2)[slot]


def whole_block(me, i):
    core = ((me >> 3) & 1) ^ ((i >> 2) & 1)
    x = ((me >> 4) & 3) ^ slot_flip(i & 3, core)
    return ((me >> 6) ^ (i >> 3)) * 8 + x * 2 + core


def feature_slot(me, i, other):
    core = ((me >> 3) & 1) ^ other
    apart = (me & 3) ^ (i & 3)
    return jnp.where(apart == 1 + 2 * core, 1, jnp.where(apart == 3 - 2 * core, 2, jnp.where(apart == 2, 3, 0)))


def call(kernel, ins, outs, scratch=(), flops=0, moved=0, mib=16, aliases={}):
    places = {"v": pltpu.VMEM, "s": pltpu.SMEM, "h": pl.ANY}
    return pl.pallas_call(
        kernel,
        in_specs=[pl.BlockSpec(memory_space=places[i]) for i in ins],
        out_specs=[pl.BlockSpec(memory_space=places[o[0]]) for o in outs],
        out_shape=[jax.ShapeDtypeStruct(o[1], o[2]) for o in outs],
        scratch_shapes=list(scratch),
        input_output_aliases=aliases,
        compiler_params=pltpu.CompilerParams(vmem_limit_bytes=mib << 20),
        cost_estimate=pl.CostEstimate(flops=flops, bytes_accessed=moved, transcendentals=0),
        name=kernel.__name__,
    )


def rows_of(i):
    return slice(32 * i, 32 * i + 32)


def from_lanes(row):
    return jnp.broadcast_to(row, (128, 128)).T


def local_block(me, i, whole):
    return whole[pl.ds(pl.multiple_of(whole_block(me, i) * 32, 32), 32), :]


def hits_of(me, ids, j):
    lane = lax.broadcasted_iota(jnp.int32, (ids.shape[0], 128), 1)
    return ids == (lane + (me * WIDTH + 128 * j)).astype(f32)


def forward(half, me_ref, *refs):
    pieces, (ids_ref, head_ref, rows, capped_ref, term_ref, total_ref, target_ref) = refs[:8], refs[8:]
    me = me_ref[0]
    for i in range(8):
        rows[rows_of(i), :] = pieces[i][...]
    ids = ids_ref[256 * half : 256 * half + 256, :]
    total = jnp.zeros((256, 128), f32)
    target = jnp.zeros((256, 128), f32)
    for n in range(4):
        raw = jnp.dot(rows[...], head_ref[:, 256 * n : 256 * n + 256], preferred_element_type=f32)
        ratio = jnp.tanh(raw / softcap)
        for j in range(2):
            start = 256 * n + 128 * j
            part = ratio[:, 128 * j : 128 * j + 128]
            capped = softcap * part
            expo = jnp.exp(capped)
            hit = hits_of(me, ids, 2 * n + j)
            capped_ref[:, start : start + 128] = capped
            term_ref[:, start : start + 128] = jnp.where(hit, 0.0, expo * (1.0 - part * part)).astype(bf16)
            total = total + expo
            target = target + jnp.where(hit, capped, 0.0)
    total_ref[...] = total
    target_ref[...] = target


def forward_low(*refs):
    forward(0, *refs)


def forward_high(*refs):
    forward(1, *refs)


def run_forward(kernel, me, pieces, ids, head):
    return call(
        kernel,
        "s" + "v" * 10,
        [
            ("v", (256, D), bf16),
            ("v", (256, WIDTH), f32),
            ("v", (256, WIDTH), bf16),
            ("v", (256, 128), f32),
            ("v", (256, 128), f32),
        ],
        flops=2 * 256 * D * WIDTH,
        moved=2 * D * WIDTH,
    )(me, *pieces, ids, head)


def pack(me_ref, total0, total1, target0, target1, out_ref, whole):
    me = me_ref[0]
    sums = []
    for halves in ((total0, total1), (target0, target1)):
        for i in range(16):
            spot = pl.ds(pl.multiple_of(whole_block(me, i) * 32, 32), 32)
            whole[spot, :] = halves[i // 8][rows_of(i % 8), :]
        for j in range(4):
            sums.append(jnp.sum(whole[128 * j : 128 * j + 128, :].T, axis=0, keepdims=True))
    out_ref[...] = jnp.concatenate(sums, axis=0)


def run_pack(me, *columns):
    return call(pack, "svvvv", [("v", (8, 128), f32)], scratch=[pltpu.VMEM(COLUMN, f32)], moved=1 << 20)(
        me, *columns
    )[0]


def unpack(me_ref, sums_ref, weight_ref, log_ref, own_ref, rest_ref, pick_ref, logs, targets):
    me = me_ref[0]
    sums = sums_ref[...]
    for j in range(4):
        logs[128 * j : 128 * j + 128, :] = from_lanes(jnp.log(sums[j : j + 1, :]))
        targets[128 * j : 128 * j + 128, :] = from_lanes(sums[4 + j : 5 + j, :])
    for i in range(16):
        log_ref[rows_of(i), :] = local_block(me, i, logs)
    own_ref[...] = local_block(me, 0, targets) - local_block(me, 0, logs)
    for zr in range(2):
        for x in range(4):
            i = 8 * zr + x
            log_total = log_ref[rows_of(i), :]
            target = local_block(me, i, targets)
            weight = weight_ref[rows_of(i), :]
            ratio = target / softcap
            rest_ref[rows_of(4 * zr + x), :] = weight * jnp.exp(-log_total)
            pick_ref[rows_of(4 * zr + x), :] = weight * (jnp.exp(target - log_total) - 1.0) * (1.0 - ratio * ratio)


def run_unpack(me, sums, weight):
    outs = [("v", COLUMN, f32), ("v", (32, 128), f32), ("v", (256, 128), f32), ("v", (256, 128), f32)]
    return call(unpack, "svv", outs, scratch=[pltpu.VMEM(COLUMN, f32)] * 2, moved=1 << 20)(me, sums, weight)


def back_part(me, n, rows, head_ref, mine_ref, mate_ref):
    out = lax.dot_general(
        rows, head_ref[1152 * n : 1152 * n + 1152, :], (((1,), (1,)), ((), ())), preferred_element_type=f32
    ).astype(bf16)
    for i in range(2):
        part = out[:, FEATURES * i : FEATURES * i + FEATURES]
        block = 2 * n + i
        spot = slice(FEATURES * (block // 4), FEATURES * (block // 4) + FEATURES)
        mine_ref[feature_slot(me, block, 0), :, :, spot] = part[:128].reshape(4, 32, FEATURES)
        mate_ref[feature_slot(me, block, 1), :, :, spot] = part[128:].reshape(4, 32, FEATURES)


def back(me_ref, rows_ref, head_ref, mine_ref, mate_ref):
    for n in range(4):
        back_part(me_ref[0], n, rows_ref[...], head_ref, mine_ref, mate_ref)


BLOCKS = ("v", (4, 4, 32, 2 * FEATURES), bf16)
BACK_COST = dict(flops=2 * 256 * D * WIDTH, moved=2 * D * WIDTH)


def run_back(me, rows, head):
    return call(back, "svv", [BLOCKS, BLOCKS], **BACK_COST)(me, rows, head)


def begin(me_ref, ids_ref, weight_ref, head_ref, mine0, mate0, mine1, mate1, held_ref, ids_out, weight_out, *scratch):
    ids_near, weight_near, ids_whole, weight_whole, rows, sems = scratch
    me = me_ref[0]
    small = [
        pltpu.make_async_copy(ids_ref, ids_near, sems.at[4]),
        pltpu.make_async_copy(weight_ref, weight_near, sems.at[5]),
    ]
    loads = []
    for n in range(4):
        spot = pl.ds(1152 * n, 1152)
        loads.append(pltpu.make_async_copy(head_ref.at[spot], held_ref.at[spot], sems.at[n]))
    for copy in small + loads:
        copy.start()
    for copy in small:
        copy.wait()
    for j in range(4):
        ids_whole[128 * j : 128 * j + 128, :] = from_lanes(ids_near[j : j + 1, :].astype(f32))
        weight_whole[128 * j : 128 * j + 128, :] = from_lanes(weight_near[j : j + 1, :])
    for i in range(16):
        ids_out[rows_of(i), :] = local_block(me, i, ids_whole)
        weight_out[rows_of(i), :] = local_block(me, i, weight_whole)
    ids = ids_out[...]
    for j in range(WIDTH // 128):
        rows[:, 128 * j : 128 * j + 128] = jnp.where(hits_of(me, ids, j), 1.0, 0.0).astype(bf16)
    for n in range(4):
        loads[n].wait()
        for half, (mine, mate) in enumerate(((mine0, mate0), (mine1, mate1))):
            back_part(me, n, rows[256 * half : 256 * half + 256, :], held_ref, mine, mate)


def run_begin(me, ids, weight, head):
    column = ("v", COLUMN, f32)
    return call(
        begin,
        "shhh",
        [BLOCKS] * 4 + [("v", (D, WIDTH), bf16), column, column],
        scratch=[
            pltpu.VMEM((4, 128), jnp.int32),
            pltpu.VMEM((4, 128), f32),
            pltpu.VMEM(COLUMN, f32),
            pltpu.VMEM(COLUMN, f32),
            pltpu.VMEM((512, WIDTH), bf16),
            pltpu.SemaphoreType.DMA((6,)),
        ],
        flops=4 * 256 * D * WIDTH,
        moved=2 * D * WIDTH,
    )(me, *(pltpu.with_memory_space_constraint(array, pltpu.HBM) for array in (ids, weight, head)))


def fold(*refs):
    parts, (p_keep, p_send, q_keep, q_send) = refs[:8], refs[8:]
    for zr in range(2):
        a_mine, a_got, g_mine, g_got = parts[4 * zr : 4 * zr + 4]
        for k in range(4):
            for x in range(4):
                p_at = (p_keep if k < 2 else p_send).at[x // 2, k % 2, x % 2, zr]
                q_at = (q_keep if x < 2 else q_send).at[k // 2, k % 2, x % 2, zr]
                for first, mine, got in ((0, a_mine, a_got), (16, g_mine, g_got)):
                    total = mine[k, x] + got[k, x]
                    p_at[first : first + 16] = total[:16]
                    q_at[first : first + 16] = total[16:]


def run_fold(*parts):
    return call(fold, "v" * 8, [("v", (2, 2, 2, 2, 32, 2 * FEATURES), bf16)] * 4, moved=512 * D * 8)(*parts)


def combine(first_row, slots, rest_ref, pick_ref, held, got, keep, out):
    for h, target in enumerate((keep, out)):
        for i in range(2):
            for j in range(2):
                x = slots(h, j)
                for zr in range(2):
                    first = 128 * zr + 32 * x + first_row
                    rest = rest_ref[first : first + 16, :]
                    pick = pick_ref[first : first + 16, :]
                    for start in range(0, 2 * FEATURES, 128):
                        at = (h, i, j, zr, slice(None), slice(start, start + 128))
                        both = (held[at] + got[at]).astype(f32)
                        target[at[1:]] = (rest * both[:16] + pick * both[16:]).astype(bf16)


def combine_p(*refs):
    combine(0, lambda h, j: 2 * h + j, *refs)


def combine_q(*refs):
    combine(16, lambda h, j: j, *refs)


def run_combine(kernel, *parts):
    half = ("v", (2, 2, 2, 16, 2 * FEATURES), bf16)
    return call(kernel, "v" * 4, [half, half], moved=1 << 22)(*parts)


def join(p_keep, p_got, q_keep, q_got, *outs):
    for n, out in enumerate(outs):
        out[:, :16] = p_keep[n // 2, n % 2] + p_got[n // 2, n % 2]
        out[:, 16:] = q_keep[n // 2, n % 2] + q_got[n // 2, n % 2]


def run_join(*parts):
    return call(join, "v" * 4, [("v", (2, 32, 2 * FEATURES), bf16)] * 4, moved=1 << 22)(*parts)


def split(me_ref, *refs):
    terms, outs = refs[:4], refs[4:]
    low = ((me_ref[0] >> 2) & 1) == 0
    for zr in range(2):
        total = sum(term[zr].astype(f32) for term in terms)
        halves = (total[:, :FEATURES], total[:, FEATURES:])
        for zl in range(2):
            outs[2 * zr + zl][...] = jnp.where(low, halves[zl], halves[1 - zl]).astype(bf16)


def run_split(me, *parts):
    return call(split, "svvvv", [("v", (32, FEATURES), bf16)] * 4, moved=1 << 20)(me, *parts)


def finish(*refs):
    terms, out_ref = refs[:4], refs[4]
    out_ref[...] = sum(term[...].astype(f32) for term in terms).astype(bf16)


def run_finish(*terms):
    return call(finish, "v" * 4, [("v", (32, FEATURES), bf16)], moved=1 << 17)(*terms)[0]


def dlogits(me_ref, low_ref, high_ref, log_ref, weight_ref, ids_ref, out_ref):
    me = me_ref[0]
    for n in range(4):
        capped_ref = low_ref if n < 2 else high_ref
        rows = slice(128 * (n % 2), 128 * (n % 2) + 128)
        out_rows = slice(128 * n, 128 * n + 128)
        log_total = log_ref[out_rows, :]
        weight = weight_ref[out_rows, :]
        ids = ids_ref[out_rows, :]
        for j in range(WIDTH // 128):
            spot = slice(128 * j, 128 * j + 128)
            capped = capped_ref[rows, spot]
            prob = jnp.exp(capped - log_total)
            onehot = jnp.where(hits_of(me, ids, j), 1.0, 0.0)
            ratio = capped / softcap
            out_ref[out_rows, spot] = (weight * (prob - onehot) * (1.0 - ratio * ratio)).astype(bf16)


def run_dlogits(me, low, high, log_total, weight, ids):
    return call(
        dlogits, "svvvvv", [("v", (512, WIDTH), bf16)], flops=512 * WIDTH * 16, moved=6 * 512 * WIDTH
    )(me, low, high, log_total, weight, ids)[0]


def head_rows(first, last, low_ref, high_ref, dlog_ref, out_ref, rows, buffer, sems):
    def copy(i):
        return pltpu.make_async_copy(buffer.at[i % 2], out_ref.at[pl.ds(512 * i, 512)], sems.at[i % 2])

    for i in range(first, last):
        spot = slice(512 * i, 512 * i + 512)
        rows[:256, :] = low_ref[:, spot]
        rows[256:, :] = high_ref[:, spot]
        if i >= first + 2:
            copy(i - 2).wait()
        buffer[i % 2] = lax.dot_general(
            rows[...], dlog_ref[...], (((0,), (0,)), ((), ())), preferred_element_type=f32
        ).astype(bf16)
        copy(i).start()
    copy(last - 2).wait()
    copy(last - 1).wait()


def head_gradient_low(low_ref, high_ref, dlog_ref, out_ref, *scratch):
    head_rows(0, 4, low_ref, high_ref, dlog_ref, out_ref, *scratch)


def head_gradient_mid(low_ref, high_ref, dlog_ref, started_ref, out_ref, *scratch):
    head_rows(4, 7, low_ref, high_ref, dlog_ref, out_ref, *scratch)


def head_gradient_high(low_ref, high_ref, dlog_ref, started_ref, out_ref, *scratch):
    head_rows(7, 9, low_ref, high_ref, dlog_ref, out_ref, *scratch)


def run_head_gradient(kernel, low, high, dlog, started=()):
    return call(
        kernel,
        "vvv" + "h" * len(started),
        [("h", (D, WIDTH), bf16)],
        scratch=[
            pltpu.VMEM((512, 512), bf16),
            pltpu.VMEM((2, 512, WIDTH), bf16),
            pltpu.SemaphoreType.DMA((2,)),
        ],
        flops=512 * WIDTH * D,
        moved=D * WIDTH,
        aliases={3: 0} if started else {},
    )(low, high, dlog, *started)[0]


def tie(*arrays):
    return lax.optimization_barrier(arrays)


def local(hidden, head, verdict_ids, row_weight):
    me = (lax.axis_index("dp") * 8 + lax.axis_index("vocab")).astype(jnp.int32).reshape(1)
    a1, a2, a3 = send(hidden, X1), send(hidden, X2), send(hidden, X3)
    o0 = send(hidden, ZH)
    g0_mine, g0_mate, g1_mine, g1_mate, head, ids, weight = run_begin(
        me, verdict_ids.reshape(4, 128), row_weight.reshape(4, 128), head
    )
    o0, a3, a2, a1, g0_mine, g0_mate, g1_mine, g1_mate = tie(o0, a3, a2, a1, g0_mine, g0_mate, g1_mine, g1_mate)
    o1, o2, o3 = send(o0, X1), send(o0, X2), send(a3, ZH)
    own_half = [hidden, a1, a2, a3]
    own_half += [send(piece, CORE) for piece in own_half]
    rows0, capped0, term0, total0, target0 = run_forward(forward_low, me, own_half, ids, head)
    o1, term0 = tie(o1, term0)
    a0_mine, a0_mate = run_back(me, term0, head)
    o1, o3, o2, a0_mate = tie(o1, o3, o2, a0_mate)
    other_half = [o0, o1, o2, o3]
    *swapped, a0_mate = tie(*(send(piece, CORE) for piece in other_half), a0_mate)
    other_half += swapped
    a0_got = send(a0_mate, CORE)
    rows1, capped1, term1, total1, target1 = run_forward(forward_high, me, other_half, ids, head)

    def step(sums, *partners):
        got = tie(*(send(sums, partner) for partner in partners))
        return sums + sum(got)

    total1, a0_got, g0_mate, g1_mate = tie(total1, a0_got, g0_mate, g1_mate)
    g0_got, g1_got = send(g0_mate, CORE), send(g1_mate, CORE)
    sums = step(run_pack(me, total0, total1, target0, target1), X1)
    a1_mine, a1_mate = run_back(me, term1, head)
    sums, a1_mate, g0_got, g1_got = tie(sums, a1_mate, g0_got, g1_got)
    a1_got = send(a1_mate, CORE)
    sums = step(sums, X2)
    a1_got, sums = tie(a1_got, sums)
    p_keep, p_send, q_keep, q_send = run_fold(
        a0_mine, a0_got, g0_mine, g0_got, a1_mine, a1_got, g1_mine, g1_got
    )
    sums = step(sums, CORE)
    p_send, q_send, sums = tie(p_send, q_send, sums)

    p_got, q_got = send(p_send, Y2), send(q_send, X2)
    sums = step(step(step(sums, ZL), ZH), Y1, Y2, Y3)
    sums, p_got, q_got = tie(sums, p_got, q_got)
    log_total, own, rest, pick = run_unpack(me, sums, weight)
    p_keep, p_send = run_combine(combine_p, rest, pick, p_keep, p_got)
    q_keep, q_send = run_combine(combine_q, rest, pick, q_keep, q_got)
    p_got, q_got = send(p_send, X2), send(q_send, Y2)
    log_total, p_keep = tie(log_total, p_keep)
    dlog = run_dlogits(me, capped0, capped1, log_total, weight, ids)
    head_grad = run_head_gradient(head_gradient_low, rows0, rows1, dlog)
    p_got, q_got, head_grad = tie(p_got, q_got, head_grad)
    keep, *outs = run_join(p_keep, p_got, q_keep, q_got)
    got = [send(out, partner) for out, partner in zip(outs, (X1, Y1, XY1))]
    head_grad = run_head_gradient(head_gradient_mid, rows0, rows1, dlog, (head_grad,))
    *got, head_grad = tie(*got, head_grad)
    keep, *outs = run_split(me, keep, *got)
    z_got = send(outs[1], Z2), send(outs[0], ZL), send(outs[2], ZH)
    head_grad = run_head_gradient(head_gradient_high, rows0, rows1, dlog, (head_grad,))
    *z_got, head_grad = tie(*z_got, head_grad)
    hidden_grad = run_finish(keep, *z_got)
    return (own[:, 0], head_grad, hidden_grad)


def solution(mesh):
    in_specs = (P("dp", None), P(None, ("dp", "vocab")), P(), P())
    out_specs = (P("dp"), P(None, ("dp", "vocab")), P("dp", "vocab"))
    return jax.shard_map(local, mesh=mesh, in_specs=in_specs, out_specs=out_specs, check_vma=False)
```
